32 devices in a mesh: row: 4 (over y, x), col: 8 (over z, core).
Axes of the slice: x: 2, y: 2, z: 4, core: 2. Of those that a mesh axis runs over, the one named last changes fastest.
Arguments:
- panel_left: bfloat16 [5000, 32, 128], P(None, ('row', 'col')), may hold values from -0.078125 to 0.078125
- panel_right: bfloat16 [5000, 32, 128], P(None, ('row', 'col')), may hold values from -6 to 6
- amplitudes: bfloat16 [128, 128, 128], P('col', 'row'), may hold values from -0.046875 to 0.046875
- eps_virtual: float32 [1600], replicated, may hold values from 0.2 to 1.5
- eps_occupied: float32 [100], replicated, may hold values from -1.5 to -0.3
- pair_list: int32 [128, 2], replicated, may hold values from 0 to 99
- blocks: int32 [2], replicated, may hold values from 0 to 49
Outputs:
- update: bfloat16 [128, 32, 32], P('col', 'row')
The draws below stay inside these ranges and needn't reach their ends.
All inputs are finite; a program needn't handle non-finite values.
Results may differ from the reference program's by a relative error of at most 0.0049.
Values may be sent and summed in bfloat16 or wider, within the bound.
A program may use at most 128 MiB of HBM per device.

```python
import jax
import jax.numpy as jnp
from jax import lax

V = 1600
NQ = 5000
NOCC = 100
CB = 128
PAIRS = 128
VWIN = 32


def place_ends(entries, own_key, least, top_value):
    longest = entries.shape.index(max(entries.shape))
    spots = []
    for shift in (0, 1):
        where = [jax.random.randint(jax.random.fold_in(own_key, axis), (), 0, length) for axis, length in enumerate(entries.shape)]
        where[longest] = (where[longest] + shift) % entries.shape[longest]
        spots.append(tuple(where))
    return entries.at[spots[0]].set(least).at[spots[1]].set(top_value)


def shard_levels(key, dims, split, least, high):
    level, own = 1.0, jax.random.fold_in(key, 6)
    for axis_at, shards_of in split:
        draws = jnp.exp(jax.random.uniform(jax.random.fold_in(own, axis_at), (shards_of,), jnp.float32, least / len(split), high / len(split)))
        level = level * jnp.repeat(draws, dims[axis_at] // shards_of).reshape([-1 if axis == axis_at else 1 for axis in range(len(dims))])
    return level


def noise(rng, shape, spread, bound, shards=(), held_as=jnp.bfloat16):
    loudness = shard_levels(rng, shape, shards, -0.22, 0.18) if shards else 1.0
    entries = jax.random.normal(rng, shape, jnp.float32) * spread * loudness
    return jnp.minimum(jnp.maximum(entries, -bound), bound).astype(held_as)


def setup_inputs(seed: int = 0) -> dict:
    keys = jax.random.split(jax.random.key(seed), 8)
    return {
        "panel_left": noise(keys[0], (NQ, VWIN, CB), NQ ** -0.5, 0.078125, ((1, 32),)),
        "panel_right": noise(keys[1], (NQ, VWIN, CB), 1.0, 6.0, ((1, 32),)),
        "amplitudes": noise(keys[2], (PAIRS, CB, CB), (CB * CB) ** -0.5, 0.046875, ((0, 8), (1, 4))),
        "eps_virtual": jnp.clip(jax.random.uniform(keys[3], (V,), jnp.float32, 0.2, 1.5), 0.2, 1.5),
        "eps_occupied": jnp.clip(jax.random.uniform(keys[4], (NOCC,), jnp.float32, -1.5, -0.3), -1.5, -0.3),
        "pair_list": place_ends(jax.random.randint(keys[5], (PAIRS, 2), 0, NOCC), jax.random.fold_in(keys[5], 1), 0, NOCC - 1).astype(jnp.int32),
        "blocks": jax.random.randint(keys[6], (2,), 0, V // VWIN).astype(jnp.int32),
    }


def reference(panel_left, panel_right, amplitudes, eps_virtual, eps_occupied, pair_list, blocks):
    right_flat = panel_right.astype(jnp.float32).reshape(NQ, VWIN * CB)
    amp_float = amplitudes.astype(jnp.float32)

    def one_row(left_slice):
        block_sum = lax.dot_general(left_slice.astype(jnp.float32), right_flat, (((0,), (0,)), ((), ())), precision=lax.Precision.HIGHEST, preferred_element_type=jnp.float32)
        rounded = lax.optimization_barrier(block_sum.astype(jnp.bfloat16))
        integrals = rounded.astype(jnp.float32).reshape(CB, VWIN, CB)
        return jnp.einsum("cbd,pcd->pb", integrals, amp_float, precision=lax.Precision.HIGHEST)

    ladder = lax.map(one_row, jnp.moveaxis(panel_left, 1, 0))
    ladder = jnp.transpose(ladder, (1, 0, 2))
    first_energy = lax.dynamic_slice_in_dim(eps_virtual, (blocks[0] * VWIN).astype(jnp.int32), VWIN)
    second_energy = lax.dynamic_slice_in_dim(eps_virtual, (blocks[1] * VWIN).astype(jnp.int32), VWIN)
    pair_sum = eps_occupied[pair_list[:, 0]] + eps_occupied[pair_list[:, 1]]
    denominator = first_energy[None, :, None] + second_energy[None, None, :] - pair_sum[:, None, None]
    return (ladder / denominator).astype(jnp.bfloat16)
```

```python
import functools

import jax
import jax.numpy as jnp
from jax import lax
from jax.experimental import pallas as pl
from jax.experimental.pallas import tpu as pltpu
from jax.sharding import PartitionSpec as P

MESH = pl.DeviceIdType.MESH
F32 = jnp.float32
BF16 = jnp.bfloat16


def arrival(ref, sem):
    pltpu.make_async_copy(ref, ref, sem).wait()


def kernel(
    row_n, col_n, qd,
    left, right, amps, eps_v, eps_o, pairs, blocks,
    out,
    lbuf, rbuf, lturn, lrows, tbuf, ybuf, acc, out1, in1, fin, out2, in2, den,
    l_send, l_recv, r_send, r_recv, t_send1, t_send2, t_send3, t_recv,
    s1_send, s1_recv, s2_send, s2_recv,
):
    n = row_n * col_n
    pairs_of_cols = col_n // 2
    slots = 2 * row_n
    cb, pb, width = amps.shape
    all_c = cb * row_n
    all_p = pb * col_n
    kp = lbuf.shape[1]
    a_own = n // row_n
    row = lax.axis_index("row")
    col = lax.axis_index("col")
    me = row * col_n + col
    cpair = col // 2
    half = col % 2

    barrier = pltpu.get_barrier_semaphore()

    def greet(e, _):
        d = (me + e) % n
        pl.semaphore_signal(barrier, inc=1, device_id=(d // col_n, d % col_n), device_id_type=MESH)
        return 0

    lax.fori_loop(1, n, greet, 0)

    def t_block(r, c):
        return tbuf.at[pl.ds(r * cb, cb), pl.ds(c * pb, pb), :]

    pltpu.make_async_copy(amps, t_block(row, col), t_recv.at[me]).start()
    pltpu.make_async_copy(
        left.at[pl.ds(me * qd, qd), :], lbuf.at[me, pl.ds(0, qd), :], l_recv.at[me]
    ).start()
    pltpu.make_async_copy(
        right.at[pl.ds(me * qd, qd), :], rbuf.at[0, row * 2 + half, pl.ds(0, qd), :], r_recv.at[me]
    ).start()

    if kp > qd:
        def clear(i, _):
            lbuf[i, pl.ds(qd, kp - qd), :] = jnp.zeros((kp - qd, width), BF16)
            rbuf[i // slots, i % slots, pl.ds(qd, kp - qd), :] = jnp.zeros((kp - qd, width), BF16)
            return 0

        lax.fori_loop(0, n, clear, 0)

    pl.semaphore_wait(barrier, n - 1)

    def mate(i):
        return 2 * ((cpair + i) % pairs_of_cols) + half

    def t1_copy(i):
        return pltpu.make_async_remote_copy(
            src_ref=amps, dst_ref=t_block(row, col),
            send_sem=t_send1.at[i], recv_sem=t_recv.at[me],
            device_id=(row, mate(i)), device_id_type=MESH,
        )

    def t2_copy(i, e):
        c = mate(i)
        return pltpu.make_async_remote_copy(
            src_ref=t_block(row, c), dst_ref=t_block(row, c),
            send_sem=t_send2.at[i * row_n + e], recv_sem=t_recv.at[row * col_n + c],
            device_id=((row + e) % row_n, col), device_id_type=MESH,
        )

    def t3_copy(i, e):
        c, r = mate(i), (row + e) % row_n
        return pltpu.make_async_remote_copy(
            src_ref=t_block(r, c), dst_ref=t_block(r, c),
            send_sem=t_send3.at[i * row_n + e], recv_sem=t_recv.at[r * col_n + c],
            device_id=(row, 2 * cpair + 1 - half), device_id_type=MESH,
        )

    def panel_copy(src, dst, d, send, recv):
        return pltpu.make_async_remote_copy(
            src_ref=src.at[pl.ds(d * qd, qd), :], dst_ref=dst,
            send_sem=send.at[d], recv_sem=recv.at[me],
            device_id=(d // col_n, d % col_n), device_id_type=MESH,
        )

    def target(k, j):
        spot = (row * 2 + half + j) % slots
        return (spot // 2) * col_n + 2 * ((cpair + pairs_of_cols - k) % pairs_of_cols) + spot % 2

    def left_copy(d):
        return panel_copy(left, lbuf.at[me, pl.ds(0, qd), :], d, l_send, l_recv)

    def right_copy(k, d):
        return panel_copy(
            right, rbuf.at[k, row * 2 + half, pl.ds(0, qd), :], d, r_send, r_recv
        )

    def phase(step):
        return (step + pairs_of_cols // 2) % pairs_of_cols

    def send_left(step):
        k = phase(step)

        def one(j, _):
            d = target(k, j)

            @pl.when(d != me)
            def _():
                left_copy(d).start()

            return 0

        lax.fori_loop(0, slots, one, 0)

    def send_right(step, _):
        k = phase(step)

        def one(j, _):
            d = target(k, j)

            @pl.when(d != me)
            def _():
                right_copy(k, d).start()

            return 0

        lax.fori_loop(0, slots, one, 0)
        return 0

    for i in range(1, pairs_of_cols):
        t1_copy(i).start()
    for step in range(pairs_of_cols):
        send_left(step)

    for i in range(pairs_of_cols):
        c = mate(i)
        arrival(t_block(row, c), t_recv.at[row * col_n + c])
        for e in range(1, row_n):
            t2_copy(i, e).start()
        t3_copy(i, 0).start()

    lax.fori_loop(0, pairs_of_cols, send_right, 0)

    span = n * a_own
    lane = lax.broadcasted_iota(jnp.int32, (pb, span), 1)
    line = lax.broadcasted_iota(jnp.int32, (pb, span), 0)
    first_at = blocks[0] * n + row * a_own
    second_at = blocks[1] * n
    first = jnp.zeros((pb, span), F32)
    for i in range(a_own):
        first = jnp.where(lane % a_own == i, eps_v[first_at + i], first)
    den[...] = first

    def add_second(b, _):
        den[...] = jnp.where(lane // a_own == b, den[...] + eps_v[second_at + b], den[...])
        return 0

    lax.fori_loop(0, n, add_second, 0)
    pair_sum = jnp.zeros((pb, span), F32)
    for i in range(pb):
        at = (col * pb + i) * 2
        level = eps_o[pairs[at]] + eps_o[pairs[at + 1]]
        pair_sum = jnp.where(line == i, level, pair_sum)
    den[...] = den[...] - pair_sum

    for e in range(1, row_n):
        for i in range(pairs_of_cols):
            r, c = (row + e) % row_n, mate(i)
            arrival(t_block(r, c), t_recv.at[r * col_n + c])
            t3_copy(i, e).start()

    def turn_left(a, _):
        arrival(lbuf.at[a, pl.ds(0, qd), :], l_recv.at[a])
        flipped = lbuf[a].astype(F32).T
        for part in range(kp // 128):
            lturn[part, pl.ds(a, all_c, stride=n), :] = flipped[:, part * 128:(part + 1) * 128]
        return 0

    lax.fori_loop(0, n, turn_left, 0)

    def pack_left(i, _):
        rows = pl.ds(pl.multiple_of(i * 128, 128), 128)
        for part in range(kp // 128):
            lrows[rows, part * 128:(part + 1) * 128] = lturn[part, rows, :].astype(BF16)
        return 0

    lax.fori_loop(0, all_c * n // 128, pack_left, 0)

    for e in range(row_n):
        for i in range(pairs_of_cols):
            r, c = (row + e) % row_n, 2 * ((cpair + i) % pairs_of_cols) + 1 - half
            arrival(t_block(r, c), t_recv.at[r * col_n + c])

    cpairs = ybuf.shape[0]
    rows_c = cpairs * 2 * n

    def s1_copy(step, e):
        r, k, slot = (row + e) % row_n, phase(step), step % 2
        return pltpu.make_async_remote_copy(
            src_ref=out1.at[slot, r], dst_ref=in1.at[k, row],
            send_sem=s1_send.at[slot * row_n + r], recv_sem=s1_recv.at[k * row_n + row],
            device_id=(r, col), device_id_type=MESH,
        )

    def chunk(step, _):
        k = phase(step)
        source = 2 * ((cpair + k) % pairs_of_cols)

        def landed(j, _):
            s = (j // 2) * col_n + source + j % 2
            arrival(rbuf.at[k, j, pl.ds(0, qd), :], r_recv.at[s])
            return 0

        lax.fori_loop(0, slots, landed, 0)
        acc[...] = jnp.zeros_like(acc)

        def some_c(ci, _):
            at = pl.multiple_of(ci * rows_c, rows_c)

            def some_b(j, _):
                weights = jnp.concatenate([rbuf[k, 2 * j], rbuf[k, 2 * j + 1]], axis=1)
                block = jnp.dot(
                    lrows[pl.ds(at, rows_c), :], weights, preferred_element_type=F32
                ).astype(BF16).reshape(cpairs, 2, n, 2 * width)
                for x in range(2):
                    spot = pl.ds(pl.multiple_of((2 * j + x) * n, n), n)
                    for h in range(2):
                        ybuf[:, spot, h * width:(h + 1) * width] = block[
                            :, h, :, x * width:(x + 1) * width
                        ]
                return 0

            lax.fori_loop(0, row_n, some_b, 0)
            total = acc[...]
            for i in range(cpairs):
                c = 2 * (ci * cpairs + i)
                total += lax.dot_general(
                    ybuf[i], jnp.concatenate([tbuf[c], tbuf[c + 1]], axis=1),
                    (((1,), (1,)), ((), ())), preferred_element_type=F32,
                )
            acc[...] = total
            return 0

        lax.fori_loop(0, all_c // (2 * cpairs), some_c, 0)
        @pl.when(step >= 2)
        def _():
            for e in range(1, row_n):
                s1_copy(step, e).wait_send()

        for r in range(row_n):
            out1[step % 2, r] = acc[...].reshape(slots, row_n, a_own, all_p)[:, r]
        for e in range(1, row_n):
            s1_copy(step, e).start()
        in1[k, row] = out1[step % 2, row]
        return 0

    lax.fori_loop(0, pairs_of_cols, chunk, 0)

    def gather_rows(step, _):
        k = phase(step)
        part = in1[k, row]
        for e in range(1, row_n):
            r = (row + e) % row_n
            arrival(in1.at[k, r], s1_recv.at[k * row_n + r])
            part += in1[k, r]
        source = 2 * ((cpair + k) % pairs_of_cols)
        for j in range(slots):
            fin[(j // 2) * col_n + source + j % 2] = part[j]
        return 0

    lax.fori_loop(0, pairs_of_cols, gather_rows, 0)
    out2[...] = fin[...].reshape(span, all_p).T

    def s2_copy(e):
        c = (col + e) % col_n
        return pltpu.make_async_remote_copy(
            src_ref=out2.at[pl.ds(c * pb, pb), :], dst_ref=in2.at[col],
            send_sem=s2_send.at[c], recv_sem=s2_recv.at[col],
            device_id=(row, c), device_id_type=MESH,
        )

    for e in range(1, col_n):
        s2_copy(e).start()
    total = out2[pl.ds(pl.multiple_of(col * pb, pb), pb), :]
    for e in range(1, col_n):
        c = (col + e) % col_n
        arrival(in2.at[c], s2_recv.at[c])
        total += in2[c]
    out[...] = (total / den[...]).astype(out.dtype)

    for i in range(1, pairs_of_cols):
        t1_copy(i).wait_send()
    for i in range(pairs_of_cols):
        for e in range(row_n):
            if e > 0:
                t2_copy(i, e).wait_send()
            t3_copy(i, e).wait_send()

    for step in range(max(0, pairs_of_cols - 2), pairs_of_cols):
        for e in range(1, row_n):
            s1_copy(step, e).wait_send()

    def drain(e, _):
        d = (me + e) % n
        left_copy(d).wait_send()
        right_copy(0, d).wait_send()
        return 0

    lax.fori_loop(1, n, drain, 0)
    for e in range(1, col_n):
        s2_copy(e).wait_send()


def shards(panel_left, panel_right, amplitudes, eps_virtual, eps_occupied, pair_list, blocks):
    row_n = lax.axis_size("row")
    col_n = lax.axis_size("col")
    n = row_n * col_n
    fit, _, width = panel_left.shape
    pb, cb, _ = amplitudes.shape
    qd = -(-fit // (16 * n)) * 16
    kp = -(-qd // 128) * 128
    pad = ((0, qd * n - fit), (0, 0))
    left = jnp.pad(panel_left.reshape(fit, width), pad)
    right = jnp.pad(panel_right.reshape(fit, width), pad)
    amps = jnp.transpose(amplitudes, (1, 0, 2))
    all_c, all_p = cb * row_n, pb * col_n
    halves = col_n // 2
    slots = 2 * row_n
    a_own = n // row_n
    span = n * a_own
    cpairs = max(1, (128 // n) ** 2)
    dma = pltpu.SemaphoreType.DMA
    hbm = pl.BlockSpec(memory_space=pl.ANY)
    smem = pl.BlockSpec(memory_space=pltpu.SMEM)
    flat = pl.pallas_call(
        functools.partial(kernel, row_n, col_n, qd),
        out_shape=jax.ShapeDtypeStruct((pb, span), BF16),
        in_specs=[hbm, hbm, hbm, smem, smem, smem, smem],
        out_specs=pl.BlockSpec(memory_space=pltpu.VMEM),
        scratch_shapes=[
            pltpu.VMEM((n, kp, width), BF16),
            pltpu.VMEM((halves, slots, kp, width), BF16),
            pltpu.VMEM((kp // 128, all_c * n, 128), F32),
            pltpu.VMEM((all_c * n, kp), BF16),
            pltpu.VMEM((all_c, all_p, width), BF16),
            pltpu.VMEM((cpairs, slots * n, 2 * width), BF16),
            pltpu.VMEM((slots * n, all_p), F32),
            pltpu.VMEM((2, row_n, slots, a_own, all_p), F32),
            pltpu.VMEM((halves, row_n, slots, a_own, all_p), F32),
            pltpu.VMEM((n, a_own, all_p), F32),
            pltpu.VMEM((all_p, span), F32),
            pltpu.VMEM((col_n, pb, span), F32),
            pltpu.VMEM((pb, span), F32),
            dma((n,)), dma((n,)), dma((n,)), dma((n,)),
            dma((halves,)), dma((halves * row_n,)), dma((halves * row_n,)), dma((n,)),
            dma((2 * row_n,)), dma((halves * row_n,)), dma((col_n,)), dma((col_n,)),
        ],
        compiler_params=pltpu.CompilerParams(
            collective_id=0, has_side_effects=True, vmem_limit_bytes=62 * 1024 * 1024
        ),
        cost_estimate=pl.CostEstimate(
            flops=2 * fit * width * width * n, bytes_accessed=4 * fit * width, transcendentals=0
        ),
        name="ladder_exchange",
    )(left, right, amps, eps_virtual, eps_occupied, pair_list.reshape(-1), blocks)
    return jnp.transpose(flat.reshape(pb, n, a_own), (0, 2, 1))


def solution(mesh):
    return jax.shard_map(
        shards,
        mesh=mesh,
        in_specs=(
            P(None, ("row", "col"), None),
            P(None, ("row", "col"), None),
            P("col", "row", None),
            P(),
            P(),
            P(),
            P(),
        ),
        out_specs=P("col", "row", None),
        check_vma=False,
    )
```

```python
import functools

import jax
import jax.numpy as jnp
from jax import lax
from jax.experimental import pallas as pl
from jax.experimental.pallas import tpu as pltpu
from jax.sharding import PartitionSpec as P

MESH = pl.DeviceIdType.MESH
F32 = jnp.float32
BF16 = jnp.bfloat16


def arrival(ref, sem):
    pltpu.make_async_copy(ref, ref, sem).wait()


def kernel(
    row_n, col_n, base, extra,
    left, right, tails, amps, eps_v, eps_o, pairs, blocks,
    out,
    lbuf, rbuf, lturn, lrows, tbuf, tturn, ybuf, acc, out1, in1, fin, out2, in2, den,
    l_send, l_recv, r_send, r_recv, t_send1, t_send2, t_send3, t_recv,
    s1_send, s1_recv, s2_send, s2_recv,
):
    n = row_n * col_n
    pairs_of_cols = col_n // 2
    slots = 2 * row_n
    cb, pb, width = amps.shape
    all_c = cb * row_n
    all_p = pb * col_n
    kp = lbuf.shape[1]
    few, most = 16 * base, 16 * (base + 1)
    a_own = n // row_n
    row = lax.axis_index("row")
    col = lax.axis_index("col")
    me = row * col_n + col
    cpair = col // 2
    half = col % 2

    barrier = pltpu.get_barrier_semaphore()

    def greet(e, _):
        d = (me + e) % n
        pl.semaphore_signal(barrier, inc=1, device_id=(d // col_n, d % col_n), device_id_type=MESH)
        return 0

    lax.fori_loop(1, n, greet, 0)

    def t_block(r, c):
        return tbuf.at[pl.ds(r * cb, cb), pl.ds(c * pb, pb), :]

    pltpu.make_async_copy(amps, t_block(row, col), t_recv.at[me]).start()

    def shares(src, which, dst, d, copy, act):
        @pl.when(d < extra)
        def _():
            act(copy(src.at[pl.ds(d * most, most), :], dst.at[pl.ds(0, most), :]))

        @pl.when((d >= extra) & (d < n - 1))
        def _():
            at = extra * most + (d - extra) * few
            act(copy(src.at[pl.ds(at, few), :], dst.at[pl.ds(0, few), :]))

        @pl.when(d == n - 1)
        def _():
            at = extra * most + (n - 1 - extra) * few
            act(copy(src.at[pl.ds(at, few - 16), :], dst.at[pl.ds(0, few - 16), :]))
            act(copy(tails.at[which], dst.at[pl.ds(few - 16, 16), :]))

    def share_arrival(ref, sem):
        @pl.when(me < extra)
        def _():
            arrival(ref.at[pl.ds(0, most), :], sem)

        @pl.when(me >= extra)
        def _():
            arrival(ref.at[pl.ds(0, few), :], sem)

    def begin(copy):
        copy.start()

    def begun(copy):
        copy.wait_send()

    shares(left, 0, lbuf.at[me], me, lambda a, b: pltpu.make_async_copy(a, b, l_recv.at[me]), begin)
    shares(
        right, 1, rbuf.at[0, row * 2 + half], me,
        lambda a, b: pltpu.make_async_copy(a, b, r_recv.at[me]), begin,
    )

    def clear(at):
        def one(i, _):
            lbuf[i, pl.ds(at, kp - at), :] = jnp.zeros((kp - at, width), BF16)
            rbuf[i // slots, i % slots, pl.ds(at, kp - at), :] = jnp.zeros((kp - at, width), BF16)
            return 0

        lax.fori_loop(0, n, one, 0)

    if kp > most:
        @pl.when(me < extra)
        def _():
            clear(most)

    @pl.when(me >= extra)
    def _():
        clear(few)

    pl.semaphore_wait(barrier, n - 1)

    def mate(i):
        return 2 * ((cpair + i) % pairs_of_cols) + half

    def t1_copy(s, up):
        c = 2 * (cpair - s if up else cpair + s) + half
        to = 2 * (cpair + 1 if up else cpair - 1) + half
        return pltpu.make_async_remote_copy(
            src_ref=t_block(row, c), dst_ref=t_block(row, c),
            send_sem=t_send1.at[2 * s + (1 if up else 0)], recv_sem=t_recv.at[row * col_n + c],
            device_id=(row, to), device_id_type=MESH,
        )

    def t1_when(s, up):
        if up:
            return (cpair >= s) & (cpair < pairs_of_cols - 1)
        return (cpair + s < pairs_of_cols) & (cpair > 0)

    def t1_step(s):
        for up in (False, True):
            if s > 0:
                @pl.when(cpair >= s if up else cpair + s < pairs_of_cols)
                def _():
                    at = row * col_n + 2 * (cpair - s if up else cpair + s) + half
                    c = 2 * (cpair - s if up else cpair + s) + half
                    arrival(t_block(row, c), t_recv.at[at])

            @pl.when(t1_when(s, up))
            def _():
                t1_copy(s, up).start()

    def t2_copy(i, e):
        c = mate(i)
        return pltpu.make_async_remote_copy(
            src_ref=t_block(row, c), dst_ref=t_block(row, c),
            send_sem=t_send2.at[i * row_n + e], recv_sem=t_recv.at[row * col_n + c],
            device_id=((row + e) % row_n, col), device_id_type=MESH,
        )

    def t3_copy(i, e):
        c, r = mate(i), (row + e) % row_n
        return pltpu.make_async_remote_copy(
            src_ref=t_block(r, c), dst_ref=t_block(r, c),
            send_sem=t_send3.at[i * row_n + e], recv_sem=t_recv.at[r * col_n + c],
            device_id=(row, 2 * cpair + 1 - half), device_id_type=MESH,
        )

    def target(k, j):
        spot = (row * 2 + half + j) % slots
        return (spot // 2) * col_n + 2 * ((cpair + pairs_of_cols - k) % pairs_of_cols) + spot % 2

    def remote(send, recv, d):
        return lambda a, b: pltpu.make_async_remote_copy(
            src_ref=a, dst_ref=b, send_sem=send.at[d], recv_sem=recv.at[me],
            device_id=(d // col_n, d % col_n), device_id_type=MESH,
        )

    def left_share(d, act):
        shares(left, 0, lbuf.at[me], d, remote(l_send, l_recv, d), act)

    def right_share(k, d, act):
        shares(right, 1, rbuf.at[k, row * 2 + half], d, remote(r_send, r_recv, d), act)

    def phase(step):
        return ((step + pairs_of_cols - 1) // pairs_of_cols) * (1 + step % (pairs_of_cols - 1))

    def send_left(j, _):
        def one(step, _):
            d = target(phase((step + 1) % pairs_of_cols), j)

            @pl.when(d != me)
            def _():
                left_share(d, begin)

            return 0

        lax.fori_loop(0, pairs_of_cols, one, 0)
        return 0

    def send_right(first, count):
        def one(i, _):
            k = phase(first + i % count)
            d = target(k, i // count)

            @pl.when(d != me)
            def _():
                right_share(k, d, begin)

            return 0

        lax.fori_loop(0, count * slots, one, 0)

    arrival(t_block(row, col), t_recv.at[me])
    for s in range(pairs_of_cols - 1):
        t1_step(s)
        lax.fori_loop(s * slots // pairs_of_cols, (s + 1) * slots // pairs_of_cols, send_left, 0)
    far = pairs_of_cols - 1
    t1_step(far)
    for i in range(pairs_of_cols):
        for e in range(1, row_n):
            t2_copy(i, e).start()
        t3_copy(i, 0).start()
    lax.fori_loop(far * slots // pairs_of_cols, slots, send_left, 0)
    send_right(0, 2)

    for e in range(1, row_n):
        for i in range(pairs_of_cols):
            r, c = (row + e) % row_n, mate(i)
            arrival(t_block(r, c), t_recv.at[r * col_n + c])
            t3_copy(i, e).start()

    for step in range(2, pairs_of_cols):
        send_right(step, 1)

    span = n * a_own
    lane = lax.broadcasted_iota(jnp.int32, (pb, span), 1)
    line = lax.broadcasted_iota(jnp.int32, (pb, span), 0)
    first_at = blocks[0] * n + row * a_own
    second_at = blocks[1] * n
    first = jnp.zeros((pb, span), F32)
    for i in range(a_own):
        first = jnp.where(lane // n == i, eps_v[first_at + i], first)
    den[...] = first

    def add_second(b, _):
        den[...] = jnp.where(lane % n == b, den[...] + eps_v[second_at + b], den[...])
        return 0

    lax.fori_loop(0, n, add_second, 0)
    pair_sum = jnp.zeros((pb, span), F32)
    for i in range(pb):
        at = col * pb + i
        level = eps_o[pairs[0, at]] + eps_o[pairs[1, at]]
        pair_sum = jnp.where(line == i, level, pair_sum)
    den[...] = den[...] - pair_sum

    for e in range(row_n):
        for i in range(pairs_of_cols):
            r, c = (row + e) % row_n, 2 * ((cpair + i) % pairs_of_cols) + 1 - half
            arrival(t_block(r, c), t_recv.at[r * col_n + c])

    def turn_amps(i, _):
        for h in range(2):
            tturn[i, h * width:(h + 1) * width, :] = tbuf[2 * i + h].astype(F32).T.astype(BF16)
        return 0

    if all_p <= width:
        lax.fori_loop(0, all_c // 2, turn_amps, 0)

    def turn_left(a, _):
        share_arrival(lbuf.at[a], l_recv.at[a])
        flipped = lbuf[a].astype(F32).T
        for part in range(kp // 128):
            lturn[part, pl.ds(a, all_c, stride=n), :] = flipped[:, part * 128:(part + 1) * 128]
        return 0

    lax.fori_loop(0, n, turn_left, 0)

    def pack_left(i, _):
        rows = pl.ds(pl.multiple_of(i * 128, 128), 128)
        for part in range(kp // 128):
            lrows[rows, part * 128:(part + 1) * 128] = lturn[part, rows, :].astype(BF16)
        return 0

    lax.fori_loop(0, all_c * n // 128, pack_left, 0)

    cpairs = ybuf.shape[0]
    rows_c = cpairs * 2 * n

    def s1_copy(step, e):
        r, k, slot = (row + e) % row_n, phase(step), step % 2
        return pltpu.make_async_remote_copy(
            src_ref=out1.at[slot, r], dst_ref=in1.at[k, row],
            send_sem=s1_send.at[slot * row_n + r], recv_sem=s1_recv.at[k * row_n + row],
            device_id=(r, col), device_id_type=MESH,
        )

    def chunk(step, _):
        k = phase(step)
        source = 2 * ((cpair + k) % pairs_of_cols)

        def landed(j, _):
            s = (j // 2) * col_n + source + j % 2
            share_arrival(rbuf.at[k, j], r_recv.at[s])
            return 0

        lax.fori_loop(0, slots, landed, 0)
        acc[...] = jnp.zeros_like(acc)

        def some_c(ci, _):
            at = pl.multiple_of(ci * rows_c, rows_c)

            def some_b(j, _):
                weights = jnp.concatenate([rbuf[k, 2 * j], rbuf[k, 2 * j + 1]], axis=1)
                block = jnp.dot(
                    lrows[pl.ds(at, rows_c), :], weights, preferred_element_type=F32
                ).astype(BF16).reshape(cpairs, 2, n, 2 * width)
                for x in range(2):
                    spot = pl.ds(pl.multiple_of((2 * j + x) * n, n), n)
                    for h in range(2):
                        ybuf[:, spot, h * width:(h + 1) * width] = block[
                            :, h, :, x * width:(x + 1) * width
                        ]
                return 0

            lax.fori_loop(0, row_n, some_b, 0)
            total = acc[...]
            for i in range(cpairs):
                at = ci * cpairs + i
                if all_p <= width:
                    total += jnp.dot(ybuf[i], tturn[at], preferred_element_type=F32)
                else:
                    amp = jnp.concatenate([tbuf[2 * at], tbuf[2 * at + 1]], axis=1)
                    total += lax.dot_general(
                        ybuf[i], amp, (((1,), (1,)), ((), ())), preferred_element_type=F32
                    )
            acc[...] = total
            return 0

        lax.fori_loop(0, all_c // (2 * cpairs), some_c, 0)
        @pl.when(step >= 2)
        def _():
            for e in range(1, row_n):
                s1_copy(step, e).wait_send()

        for r in range(row_n):
            out1[step % 2, r] = acc[...].reshape(slots, row_n, a_own, all_p)[:, r]
        for e in range(1, row_n):
            s1_copy(step, e).start()
        in1[k, row] = out1[step % 2, row]
        return 0

    lax.fori_loop(0, pairs_of_cols, chunk, 0)

    def gather_rows(step, _):
        k = phase(step)
        part = in1[k, row]
        for e in range(1, row_n):
            r = (row + e) % row_n
            arrival(in1.at[k, r], s1_recv.at[k * row_n + r])
            part += in1[k, r]
        source = 2 * ((cpair + k) % pairs_of_cols)
        for j in range(slots):
            b = (j // 2) * col_n + source + j % 2
            for x in range(all_p // 128):
                fin[x, pl.ds(b, a_own, stride=n), :] = part[j, :, x * 128:(x + 1) * 128]
        return 0

    lax.fori_loop(0, pairs_of_cols, gather_rows, 0)
    for x in range(all_p // 128):
        out2[x * 128:(x + 1) * 128, :] = fin[x].T

    def s2_copy(e):
        c = (col + e) % col_n
        return pltpu.make_async_remote_copy(
            src_ref=out2.at[pl.ds(c * pb, pb), :], dst_ref=in2.at[col],
            send_sem=s2_send.at[c], recv_sem=s2_recv.at[col],
            device_id=(row, c), device_id_type=MESH,
        )

    for e in range(1, col_n):
        s2_copy(e).start()
    total = out2[pl.ds(pl.multiple_of(col * pb, pb), pb), :]
    for e in range(1, col_n):
        c = (col + e) % col_n
        arrival(in2.at[c], s2_recv.at[c])
        total += in2[c]
    out[...] = (total / den[...]).astype(out.dtype)

    for s in range(pairs_of_cols):
        for up in (False, True):
            @pl.when(t1_when(s, up))
            def _():
                t1_copy(s, up).wait_send()

    for i in range(pairs_of_cols):
        for e in range(row_n):
            if e > 0:
                t2_copy(i, e).wait_send()
            t3_copy(i, e).wait_send()

    for step in range(max(0, pairs_of_cols - 2), pairs_of_cols):
        for e in range(1, row_n):
            s1_copy(step, e).wait_send()

    def drain(e, _):
        d = (me + e) % n
        left_share(d, begun)
        right_share(0, d, begun)
        return 0

    lax.fori_loop(1, n, drain, 0)
    for e in range(1, col_n):
        s2_copy(e).wait_send()


def shards(panel_left, panel_right, amplitudes, eps_virtual, eps_occupied, pair_list, blocks):
    row_n = lax.axis_size("row")
    col_n = lax.axis_size("col")
    n = row_n * col_n
    fit, _, width = panel_left.shape
    pb, cb, _ = amplitudes.shape
    units = -(-fit // 16)
    base, extra = units // n, units % n
    kp = -(-16 * (base + 1) // 128) * 128
    left = panel_left.reshape(fit, width)
    right = panel_right.reshape(fit, width)
    last = 16 * (units - 1)
    tails = jnp.pad(jnp.stack([left[last:], right[last:]]), ((0, 0), (0, 16 * units - fit), (0, 0)))
    amps = jnp.transpose(amplitudes, (1, 0, 2))
    all_c, all_p = cb * row_n, pb * col_n
    halves = col_n // 2
    slots = 2 * row_n
    a_own = n // row_n
    span = n * a_own
    cpairs = max(1, (128 // n) ** 2)
    dma = pltpu.SemaphoreType.DMA
    hbm = pl.BlockSpec(memory_space=pl.ANY)
    smem = pl.BlockSpec(memory_space=pltpu.SMEM)
    flat = pl.pallas_call(
        functools.partial(kernel, row_n, col_n, base, extra),
        out_shape=jax.ShapeDtypeStruct((pb, span), BF16),
        in_specs=[hbm, hbm, hbm, hbm, smem, smem, smem, smem],
        out_specs=pl.BlockSpec(memory_space=pltpu.VMEM),
        scratch_shapes=[
            pltpu.VMEM((n, kp, width), BF16),
            pltpu.VMEM((halves, slots, kp, width), BF16),
            pltpu.VMEM((kp // 128, all_c * n, 128), F32),
            pltpu.VMEM((all_c * n, kp), BF16),
            pltpu.VMEM((all_c, all_p, width), BF16),
            pltpu.VMEM((all_c // 2 if all_p <= width else 1, 2 * width, all_p), BF16),
            pltpu.VMEM((cpairs, slots * n, 2 * width), BF16),
            pltpu.VMEM((slots * n, all_p), F32),
            pltpu.VMEM((2, row_n, slots, a_own, all_p), F32),
            pltpu.VMEM((halves, row_n, slots, a_own, all_p), F32),
            pltpu.VMEM((all_p // 128, span, 128), F32),
            pltpu.VMEM((all_p, span), F32),
            pltpu.VMEM((col_n, pb, span), F32),
            pltpu.VMEM((pb, span), F32),
            dma((n,)), dma((n,)), dma((n,)), dma((n,)),
            dma((2 * halves,)), dma((halves * row_n,)), dma((halves * row_n,)), dma((n,)),
            dma((2 * row_n,)), dma((halves * row_n,)), dma((col_n,)), dma((col_n,)),
        ],
        compiler_params=pltpu.CompilerParams(
            collective_id=0, has_side_effects=True, vmem_limit_bytes=62 * 1024 * 1024
        ),
        cost_estimate=pl.CostEstimate(
            flops=2 * fit * width * width * n, bytes_accessed=4 * fit * width, transcendentals=0
        ),
        name="ladder_exchange",
    )(left, right, tails, amps, eps_virtual, eps_occupied, pair_list.T, blocks)
    return flat.reshape(pb, a_own, n)


def solution(mesh):
    return jax.shard_map(
        shards,
        mesh=mesh,
        in_specs=(
            P(None, ("row", "col"), None),
            P(None, ("row", "col"), None),
            P("col", "row", None),
            P(),
            P(),
            P(),
            P(),
        ),
        out_specs=P("col", "row", None),
        check_vma=False,
    )
```

```python
import functools

import jax
import jax.numpy as jnp
from jax import lax
from jax.experimental import pallas as pl
from jax.experimental.pallas import tpu as pltpu
from jax.sharding import PartitionSpec as P

MESH = pl.DeviceIdType.MESH
F32 = jnp.float32
BF16 = jnp.bfloat16


def arrival(ref, sem):
    pltpu.make_async_copy(ref, ref, sem).wait()


def kernel(
    row_n, col_n, base, extra,
    left, right, tails, amps, eps_v, eps_o, pairs, blocks,
    out,
    lbuf, rbuf, lturn, lrows, tbuf, tturn, ybuf, acc, out1, in1, fin, out2, in2, den,
    l_send, l_recv, r_send, r_recv, t_send1, t_send2, t_send3, t_recv,
    s1_send, s1_recv, s2_send, s2_recv,
):
    n = row_n * col_n
    pairs_of_cols = col_n // 2
    slots = 2 * row_n
    cb, pb, width = amps.shape
    all_c = cb * row_n
    all_p = pb * col_n
    kp = lbuf.shape[1]
    few, most = 16 * base, 16 * (base + 1)
    a_own = n // row_n
    row = lax.axis_index("row")
    col = lax.axis_index("col")
    me = row * col_n + col
    cpair = col // 2
    half = col % 2

    barrier = pltpu.get_barrier_semaphore()

    def greet(e, _):
        d = (me + e) % n
        pl.semaphore_signal(barrier, inc=1, device_id=(d // col_n, d % col_n), device_id_type=MESH)
        return 0

    lax.fori_loop(1, n, greet, 0)

    def t_block(r, c):
        return tbuf.at[pl.ds(r * cb, cb), pl.ds(c * pb, pb), :]

    pltpu.make_async_copy(amps, t_block(row, col), t_recv.at[me]).start()

    def shares(src, which, dst, d, copy, act):
        @pl.when(d < extra)
        def _():
            act(copy(src.at[pl.ds(d * most, most), :], dst.at[pl.ds(0, most), :]))

        @pl.when((d >= extra) & (d < n - 1))
        def _():
            at = extra * most + (d - extra) * few
            act(copy(src.at[pl.ds(at, few), :], dst.at[pl.ds(0, few), :]))

        @pl.when(d == n - 1)
        def _():
            at = extra * most + (n - 1 - extra) * few
            act(copy(src.at[pl.ds(at, few - 16), :], dst.at[pl.ds(0, few - 16), :]))
            act(copy(tails.at[which], dst.at[pl.ds(few - 16, 16), :]))

    def share_arrival(ref, sem):
        @pl.when(me < extra)
        def _():
            arrival(ref.at[pl.ds(0, most), :], sem)

        @pl.when(me >= extra)
        def _():
            arrival(ref.at[pl.ds(0, few), :], sem)

    def begin(copy):
        copy.start()

    def begun(copy):
        copy.wait_send()

    shares(left, 0, lbuf.at[me], me, lambda a, b: pltpu.make_async_copy(a, b, l_recv.at[me]), begin)
    shares(
        right, 1, rbuf.at[0, row * 2 + half], me,
        lambda a, b: pltpu.make_async_copy(a, b, r_recv.at[me]), begin,
    )

    def clear(at):
        def one(i, _):
            lbuf[i, pl.ds(at, kp - at), :] = jnp.zeros((kp - at, width), BF16)
            rbuf[i // slots, i % slots, pl.ds(at, kp - at), :] = jnp.zeros((kp - at, width), BF16)
            return 0

        lax.fori_loop(0, n, one, 0)

    if kp > most:
        @pl.when(me < extra)
        def _():
            clear(most)

    @pl.when(me >= extra)
    def _():
        clear(few)

    pl.semaphore_wait(barrier, n - 1)

    def mate(i):
        return 2 * ((cpair + i) % pairs_of_cols) + half

    def t1_copy(i):
        return pltpu.make_async_remote_copy(
            src_ref=amps, dst_ref=t_block(row, col),
            send_sem=t_send1.at[i], recv_sem=t_recv.at[me],
            device_id=(row, mate(i)), device_id_type=MESH,
        )

    def t2_copy(i, e):
        c = mate(i)
        return pltpu.make_async_remote_copy(
            src_ref=t_block(row, c), dst_ref=t_block(row, c),
            send_sem=t_send2.at[i * row_n + e], recv_sem=t_recv.at[row * col_n + c],
            device_id=((row + e) % row_n, col), device_id_type=MESH,
        )

    def t3_copy(i, e):
        c, r = mate(i), (row + e) % row_n
        return pltpu.make_async_remote_copy(
            src_ref=t_block(r, c), dst_ref=t_block(r, c),
            send_sem=t_send3.at[i * row_n + e], recv_sem=t_recv.at[r * col_n + c],
            device_id=(row, 2 * cpair + 1 - half), device_id_type=MESH,
        )

    def target(k, j):
        spot = (row * 2 + half + j) % slots
        return (spot // 2) * col_n + 2 * ((cpair + pairs_of_cols - k) % pairs_of_cols) + spot % 2

    def remote(send, recv, d):
        return lambda a, b: pltpu.make_async_remote_copy(
            src_ref=a, dst_ref=b, send_sem=send.at[d], recv_sem=recv.at[me],
            device_id=(d // col_n, d % col_n), device_id_type=MESH,
        )

    def left_share(d, act):
        shares(left, 0, lbuf.at[me], d, remote(l_send, l_recv, d), act)

    def right_share(k, d, act):
        shares(right, 1, rbuf.at[k, row * 2 + half], d, remote(r_send, r_recv, d), act)

    def phase(step):
        return ((step + pairs_of_cols - 1) // pairs_of_cols) * (1 + step % (pairs_of_cols - 1))

    def send_left(j, _):
        def one(step, _):
            d = target(phase((step + 1) % pairs_of_cols), j)

            @pl.when(d != me)
            def _():
                left_share(d, begin)

            return 0

        lax.fori_loop(0, pairs_of_cols, one, 0)
        return 0

    def send_right(first, count):
        def one(i, _):
            k = phase(first + i % count)
            d = target(k, i // count)

            @pl.when(d != me)
            def _():
                right_share(k, d, begin)

            return 0

        lax.fori_loop(0, count * slots, one, 0)

    for i in range(1, pairs_of_cols):
        t1_copy(i).start()
    lax.fori_loop(0, slots // 2, send_left, 0)
    for i in range(pairs_of_cols):
        c = mate(i)
        arrival(t_block(row, c), t_recv.at[row * col_n + c])
        for e in range(1, row_n):
            t2_copy(i, e).start()
        t3_copy(i, 0).start()
    lax.fori_loop(slots // 2, slots, send_left, 0)
    send_right(0, 2)

    for e in range(1, row_n):
        for i in range(pairs_of_cols):
            r, c = (row + e) % row_n, mate(i)
            arrival(t_block(r, c), t_recv.at[r * col_n + c])
            t3_copy(i, e).start()

    for step in range(2, pairs_of_cols):
        send_right(step, 1)

    span = n * a_own
    lane = lax.broadcasted_iota(jnp.int32, (pb, span), 1)
    line = lax.broadcasted_iota(jnp.int32, (pb, span), 0)
    first_at = blocks[0] * n + row * a_own
    second_at = blocks[1] * n
    first = jnp.zeros((pb, span), F32)
    for i in range(a_own):
        first = jnp.where(lane // n == i, eps_v[first_at + i], first)
    den[...] = first

    def add_second(b, _):
        den[...] = jnp.where(lane % n == b, den[...] + eps_v[second_at + b], den[...])
        return 0

    lax.fori_loop(0, n, add_second, 0)
    pair_sum = jnp.zeros((pb, span), F32)
    for i in range(pb):
        at = col * pb + i
        level = eps_o[pairs[0, at]] + eps_o[pairs[1, at]]
        pair_sum = jnp.where(line == i, level, pair_sum)
    den[...] = den[...] - pair_sum

    def turn_left(a, _):
        share_arrival(lbuf.at[a], l_recv.at[a])
        flipped = lbuf[a].astype(F32).T
        for part in range(kp // 128):
            lturn[part, pl.ds(a, all_c, stride=n), :] = flipped[:, part * 128:(part + 1) * 128]
        return 0

    lax.fori_loop(0, n, turn_left, 0)

    def pack_left(i, _):
        rows = pl.ds(pl.multiple_of(i * 128, 128), 128)
        for part in range(kp // 128):
            lrows[rows, part * 128:(part + 1) * 128] = lturn[part, rows, :].astype(BF16)
        return 0

    lax.fori_loop(0, all_c * n // 128, pack_left, 0)

    c_step = ybuf.shape[2] // width
    rows_c = c_step * n
    block_rows = slots * n
    early = ybuf.shape[0] > 1

    def take_amps():
        for e in range(row_n):
            for i in range(pairs_of_cols):
                r, c = (row + e) % row_n, 2 * ((cpair + i) % pairs_of_cols) + 1 - half
                arrival(t_block(r, c), t_recv.at[r * col_n + c])

        def turn_amps(i, _):
            for h in range(4):
                at = pl.multiple_of((4 * i + h) * width, width)
                tturn[pl.ds(at, width), :] = tbuf[4 * i + h].astype(F32).T.astype(BF16)
            return 0

        if early:
            lax.fori_loop(0, all_c // 4, turn_amps, 0)

    def s1_copy(step, e):
        r, k, slot = (row + e) % row_n, phase(step), step % 2
        return pltpu.make_async_remote_copy(
            src_ref=out1.at[slot, r], dst_ref=in1.at[k, row],
            send_sem=s1_send.at[slot * row_n + r], recv_sem=s1_recv.at[k * row_n + row],
            device_id=(r, col), device_id_type=MESH,
        )

    def land(step):
        k = phase(step)
        source = 2 * ((cpair + k) % pairs_of_cols)

        def landed(j, _):
            s = (j // 2) * col_n + source + j % 2
            share_arrival(rbuf.at[k, j], r_recv.at[s])
            return 0

        lax.fori_loop(0, slots, landed, 0)

    def integrals(step, ci, lead, first_row):
        k = phase(step)
        at = pl.multiple_of(ci * rows_c, rows_c)

        def some_b(j, _):
            weights = jnp.concatenate([rbuf[k, 2 * j], rbuf[k, 2 * j + 1]], axis=1)
            block = jnp.dot(
                lrows[pl.ds(at, rows_c), :], weights, preferred_element_type=F32
            ).astype(BF16).reshape(c_step, n, 2 * width)
            for x in range(2):
                spot = pl.ds(pl.multiple_of(first_row + (2 * j + x) * n, n), n)
                for c in range(c_step):
                    ybuf[lead, spot, c * width:(c + 1) * width] = block[
                        c, :, x * width:(x + 1) * width
                    ]
            return 0

        lax.fori_loop(0, row_n, some_b, 0)

    def emit(step, first_row):
        @pl.when(step >= 2)
        def _():
            for e in range(1, row_n):
                s1_copy(step, e).wait_send()

        part = acc[pl.ds(first_row, block_rows), :].reshape(slots, row_n, a_own, all_p)
        for r in range(row_n):
            out1[step % 2, r] = part[:, r]
        for e in range(1, row_n):
            s1_copy(step, e).start()
        in1[phase(step), row] = out1[step % 2, row]

    def all_integrals(step, _):
        land(step)
        first_row = pl.multiple_of(step * block_rows, block_rows)

        def some_c(ci, _):
            integrals(step, ci, ci, first_row)
            return 0

        lax.fori_loop(0, all_c // c_step, some_c, 0)
        return 0

    def ladder(first_row, rows):
        acc[pl.ds(0, rows), :] = jnp.zeros((rows, all_p), F32)

        def some_c(ci, _):
            depth = c_step * width
            at = pl.multiple_of(ci * depth, depth)
            acc[pl.ds(0, rows), :] += jnp.dot(
                ybuf[ci, pl.ds(first_row, rows), :], tturn[pl.ds(at, depth), :],
                preferred_element_type=F32,
            )
            return 0

        lax.fori_loop(0, all_c // c_step, some_c, 0)

    def chunk(step, _):
        land(step)
        acc[...] = jnp.zeros_like(acc)

        def some_c(ci, _):
            integrals(step, ci, 0, 0)
            amp = jnp.concatenate([tbuf[c_step * ci + c] for c in range(c_step)], axis=1)
            acc[...] += lax.dot_general(
                ybuf[0], amp, (((1,), (1,)), ((), ())), preferred_element_type=F32
            )
            return 0

        lax.fori_loop(0, all_c // c_step, some_c, 0)
        emit(step, 0)
        return 0

    if early:
        lax.fori_loop(0, 2, all_integrals, 0)
        take_amps()
        ladder(0, 2 * block_rows)
        for step in range(2):
            emit(step, step * block_rows)

        def later(step, _):
            all_integrals(step, 0)
            ladder(pl.multiple_of(step * block_rows, block_rows), block_rows)
            emit(step, 0)
            return 0

        lax.fori_loop(2, pairs_of_cols, later, 0)
    else:
        take_amps()
        lax.fori_loop(0, pairs_of_cols, chunk, 0)

    def gather_rows(step, _):
        k = phase(step)
        part = in1[k, row]
        for e in range(1, row_n):
            r = (row + e) % row_n
            arrival(in1.at[k, r], s1_recv.at[k * row_n + r])
            part += in1[k, r]
        source = 2 * ((cpair + k) % pairs_of_cols)
        for j in range(slots):
            b = (j // 2) * col_n + source + j % 2
            for x in range(all_p // 128):
                fin[x, pl.ds(b, a_own, stride=n), :] = part[j, :, x * 128:(x + 1) * 128]
        return 0

    lax.fori_loop(0, pairs_of_cols, gather_rows, 0)
    for x in range(all_p // 128):
        out2[x * 128:(x + 1) * 128, :] = fin[x].T

    def s2_copy(e):
        c = (col + e) % col_n
        return pltpu.make_async_remote_copy(
            src_ref=out2.at[pl.ds(c * pb, pb), :], dst_ref=in2.at[col],
            send_sem=s2_send.at[c], recv_sem=s2_recv.at[col],
            device_id=(row, c), device_id_type=MESH,
        )

    for e in range(1, col_n):
        s2_copy(e).start()
    total = out2[pl.ds(pl.multiple_of(col * pb, pb), pb), :]
    for e in range(1, col_n):
        c = (col + e) % col_n
        arrival(in2.at[c], s2_recv.at[c])
        total += in2[c]
    out[...] = (total / den[...]).astype(out.dtype)

    for i in range(1, pairs_of_cols):
        t1_copy(i).wait_send()
    for i in range(pairs_of_cols):
        for e in range(row_n):
            if e > 0:
                t2_copy(i, e).wait_send()
            t3_copy(i, e).wait_send()

    for step in range(max(0, pairs_of_cols - 2), pairs_of_cols):
        for e in range(1, row_n):
            s1_copy(step, e).wait_send()

    def drain(e, _):
        d = (me + e) % n
        left_share(d, begun)
        right_share(0, d, begun)
        return 0

    lax.fori_loop(1, n, drain, 0)
    for e in range(1, col_n):
        s2_copy(e).wait_send()


def shards(panel_left, panel_right, amplitudes, eps_virtual, eps_occupied, pair_list, blocks):
    row_n = lax.axis_size("row")
    col_n = lax.axis_size("col")
    n = row_n * col_n
    fit, _, width = panel_left.shape
    pb, cb, _ = amplitudes.shape
    units = -(-fit // 16)
    base, extra = units // n, units % n
    kp = -(-16 * (base + 1) // 128) * 128
    left = panel_left.reshape(fit, width)
    right = panel_right.reshape(fit, width)
    last = 16 * (units - 1)
    tails = jnp.pad(jnp.stack([left[last:], right[last:]]), ((0, 0), (0, 16 * units - fit), (0, 0)))
    amps = jnp.transpose(amplitudes, (1, 0, 2))
    all_c, all_p = cb * row_n, pb * col_n
    halves = col_n // 2
    slots = 2 * row_n
    a_own = n // row_n
    span = n * a_own
    early = all_c * n * n * width <= 2 ** 24 and all_p <= width
    c_step = 32 if early else 2
    dma = pltpu.SemaphoreType.DMA
    hbm = pl.BlockSpec(memory_space=pl.ANY)
    smem = pl.BlockSpec(memory_space=pltpu.SMEM)
    flat = pl.pallas_call(
        functools.partial(kernel, row_n, col_n, base, extra),
        out_shape=jax.ShapeDtypeStruct((pb, span), BF16),
        in_specs=[hbm, hbm, hbm, hbm, smem, smem, smem, smem],
        out_specs=pl.BlockSpec(memory_space=pltpu.VMEM),
        scratch_shapes=[
            pltpu.VMEM((n, kp, width), BF16),
            pltpu.VMEM((halves, slots, kp, width), BF16),
            pltpu.VMEM((kp // 128, all_c * n, 128), F32),
            pltpu.VMEM((all_c * n, kp), BF16),
            pltpu.VMEM((all_c, all_p, width), BF16),
            pltpu.VMEM((all_c * width if early else 16, all_p), BF16),
            pltpu.VMEM(
                (all_c // c_step, n * n, c_step * width) if early else (1, slots * n, c_step * width),
                BF16,
            ),
            pltpu.VMEM((2 * slots * n if early else slots * n, all_p), F32),
            pltpu.VMEM((2, row_n, slots, a_own, all_p), F32),
            pltpu.VMEM((halves, row_n, slots, a_own, all_p), F32),
            pltpu.VMEM((all_p // 128, span, 128), F32),
            pltpu.VMEM((all_p, span), F32),
            pltpu.VMEM((col_n, pb, span), F32),
            pltpu.VMEM((pb, span), F32),
            dma((n,)), dma((n,)), dma((n,)), dma((n,)),
            dma((halves,)), dma((halves * row_n,)), dma((halves * row_n,)), dma((n,)),
            dma((2 * row_n,)), dma((halves * row_n,)), dma((col_n,)), dma((col_n,)),
        ],
        compiler_params=pltpu.CompilerParams(
            collective_id=0, has_side_effects=True, vmem_limit_bytes=62 * 1024 * 1024
        ),
        cost_estimate=pl.CostEstimate(
            flops=2 * fit * width * width * n, bytes_accessed=4 * fit * width, transcendentals=0
        ),
        name="ladder_exchange",
    )(left, right, tails, amps, eps_virtual, eps_occupied, pair_list.T, blocks)
    return flat.reshape(pb, a_own, n)


def solution(mesh):
    return jax.shard_map(
        shards,
        mesh=mesh,
        in_specs=(
            P(None, ("row", "col"), None),
            P(None, ("row", "col"), None),
            P("col", "row", None),
            P(),
            P(),
            P(),
            P(),
        ),
        out_specs=P("col", "row", None),
        check_vma=False,
    )
```

```python
import functools

import jax
import jax.numpy as jnp
from jax import lax
from jax.experimental import pallas as pl
from jax.experimental.pallas import tpu as pltpu
from jax.sharding import PartitionSpec as P

MESH = pl.DeviceIdType.MESH
F32 = jnp.float32
BF16 = jnp.bfloat16


def arrival(ref, sem):
    pltpu.make_async_copy(ref, ref, sem).wait()


def kernel(
    row_n, col_n, base, extra,
    left, right, tails, amps, eps_v, eps_o, pairs, blocks,
    out,
    lbuf, rbuf, lturn, lrows, tbuf, tturn, ybuf, acc, out1, in1, fin, out2, in2, den,
    l_send, l_recv, r_send, r_recv, t_send1, t_send2, t_send3, t_recv,
    s1_send, s1_recv, s2_send, s2_recv,
):
    n = row_n * col_n
    pairs_of_cols = col_n // 2
    slots = 2 * row_n
    cb, pb, width = amps.shape
    all_c = cb * row_n
    all_p = pb * col_n
    kp = lbuf.shape[1]
    few, most = 16 * base, 16 * (base + 1)
    a_own = n // row_n
    row = lax.axis_index("row")
    col = lax.axis_index("col")
    me = row * col_n + col
    cpair = col // 2
    half = col % 2

    barrier = pltpu.get_barrier_semaphore()

    def greet(e, _):
        d = (me + e) % n
        pl.semaphore_signal(barrier, inc=1, device_id=(d // col_n, d % col_n), device_id_type=MESH)
        return 0

    lax.fori_loop(1, n, greet, 0)

    def t_block(r, c):
        return tbuf.at[pl.ds(r * cb, cb), pl.ds(c * pb, pb), :]

    pltpu.make_async_copy(amps, t_block(row, col), t_recv.at[me]).start()

    def shares(src, which, dst, d, copy, act):
        @pl.when(d < extra)
        def _():
            act(copy(src.at[pl.ds(d * most, most), :], dst.at[pl.ds(0, most), :]))

        @pl.when((d >= extra) & (d < n - 1))
        def _():
            at = extra * most + (d - extra) * few
            act(copy(src.at[pl.ds(at, few), :], dst.at[pl.ds(0, few), :]))

        @pl.when(d == n - 1)
        def _():
            at = extra * most + (n - 1 - extra) * few
            act(copy(src.at[pl.ds(at, few - 16), :], dst.at[pl.ds(0, few - 16), :]))
            act(copy(tails.at[which], dst.at[pl.ds(few - 16, 16), :]))

    def share_arrival(ref, sem):
        @pl.when(me < extra)
        def _():
            arrival(ref.at[pl.ds(0, most), :], sem)

        @pl.when(me >= extra)
        def _():
            arrival(ref.at[pl.ds(0, few), :], sem)

    def begin(copy):
        copy.start()

    def begun(copy):
        copy.wait_send()

    shares(left, 0, lbuf.at[me], me, lambda a, b: pltpu.make_async_copy(a, b, l_recv.at[me]), begin)
    shares(
        right, 1, rbuf.at[0, row * 2 + half], me,
        lambda a, b: pltpu.make_async_copy(a, b, r_recv.at[me]), begin,
    )

    def clear(at):
        def one(i, _):
            lbuf[i, pl.ds(at, kp - at), :] = jnp.zeros((kp - at, width), BF16)
            rbuf[i // slots, i % slots, pl.ds(at, kp - at), :] = jnp.zeros((kp - at, width), BF16)
            return 0

        lax.fori_loop(0, n, one, 0)

    if kp > most:
        @pl.when(me < extra)
        def _():
            clear(most)

    @pl.when(me >= extra)
    def _():
        clear(few)

    pl.semaphore_wait(barrier, n - 1)

    def mate(i):
        other, bit = cpair, 1
        while bit <= i:
            if i & bit:
                other = other + bit * (1 - 2 * ((other // bit) % 2))
            bit *= 2
        return 2 * other + half

    hops, bit, held = [], pairs_of_cols // 2, [0]
    while bit:
        hops += [(block, bit) for block in held]
        held += [block + bit for block in held]
        bit //= 2

    def t1_copy(i):
        block, partner = hops[i]
        c = mate(block)
        return pltpu.make_async_remote_copy(
            src_ref=t_block(row, c), dst_ref=t_block(row, c),
            send_sem=t_send1.at[i], recv_sem=t_recv.at[row * col_n + c],
            device_id=(row, mate(partner)), device_id_type=MESH,
        )

    def t2_copy(i, e):
        c = mate(i)
        return pltpu.make_async_remote_copy(
            src_ref=t_block(row, c), dst_ref=t_block(row, c),
            send_sem=t_send2.at[i * row_n + e], recv_sem=t_recv.at[row * col_n + c],
            device_id=((row + e) % row_n, col), device_id_type=MESH,
        )

    def t3_copy(i, e):
        c, r = mate(i), (row + e) % row_n
        return pltpu.make_async_remote_copy(
            src_ref=t_block(r, c), dst_ref=t_block(r, c),
            send_sem=t_send3.at[i * row_n + e], recv_sem=t_recv.at[r * col_n + c],
            device_id=(row, 2 * cpair + 1 - half), device_id_type=MESH,
        )

    def target(k, j):
        spot = (row * 2 + half + j) % slots
        return (spot // 2) * col_n + 2 * ((cpair + pairs_of_cols - k) % pairs_of_cols) + spot % 2

    def remote(send, recv, d):
        return lambda a, b: pltpu.make_async_remote_copy(
            src_ref=a, dst_ref=b, send_sem=send.at[d], recv_sem=recv.at[me],
            device_id=(d // col_n, d % col_n), device_id_type=MESH,
        )

    def left_share(d, act):
        shares(left, 0, lbuf.at[me], d, remote(l_send, l_recv, d), act)

    def right_share(k, d, act):
        shares(right, 1, rbuf.at[k, row * 2 + half], d, remote(r_send, r_recv, d), act)

    def phase(step):
        return ((step + pairs_of_cols - 1) // pairs_of_cols) * (1 + step % (pairs_of_cols - 1))

    def send_left(j, _):
        def one(step, _):
            d = target(phase((step + 1) % pairs_of_cols), j)

            @pl.when(d != me)
            def _():
                left_share(d, begin)

            return 0

        lax.fori_loop(0, pairs_of_cols, one, 0)
        return 0

    def send_right(first, count):
        def one(i, _):
            k = phase(first + i % count)
            d = target(k, i // count)

            @pl.when(d != me)
            def _():
                right_share(k, d, begin)

            return 0

        lax.fori_loop(0, count * slots, one, 0)

    here = set()

    def need(block):
        if block not in here:
            here.add(block)
            c = mate(block)
            arrival(t_block(row, c), t_recv.at[row * col_n + c])

    for own in (True, False):
        for i, (block, _) in enumerate(hops):
            if (block == 0) == own:
                need(block)
                t1_copy(i).start()
        lax.fori_loop(0 if own else slots // 4, slots // 4 if own else slots // 2, send_left, 0)
    for i in range(pairs_of_cols):
        need(i)
        for e in range(1, row_n):
            t2_copy(i, e).start()
        t3_copy(i, 0).start()
    lax.fori_loop(slots // 2, slots, send_left, 0)
    send_right(0, 2)
    if pairs_of_cols > 2:
        send_right(2, 1)

    for e in range(1, row_n):
        for i in range(pairs_of_cols):
            r, c = (row + e) % row_n, mate(i)
            arrival(t_block(r, c), t_recv.at[r * col_n + c])
            t3_copy(i, e).start()

    for step in range(3, pairs_of_cols):
        send_right(step, 1)

    span = n * a_own
    lane = lax.broadcasted_iota(jnp.int32, (pb, span), 1)
    line = lax.broadcasted_iota(jnp.int32, (pb, span), 0)
    first_at = blocks[0] * n + row * a_own
    second_at = blocks[1] * n
    first = jnp.zeros((pb, span), F32)
    for i in range(a_own):
        first = jnp.where(lane // n == i, eps_v[first_at + i], first)
    den[...] = first

    def add_second(b, _):
        den[...] = jnp.where(lane % n == b, den[...] + eps_v[second_at + b], den[...])
        return 0

    lax.fori_loop(0, n, add_second, 0)
    pair_sum = jnp.zeros((pb, span), F32)
    for i in range(pb):
        at = col * pb + i
        level = eps_o[pairs[0, at]] + eps_o[pairs[1, at]]
        pair_sum = jnp.where(line == i, level, pair_sum)
    den[...] = den[...] - pair_sum

    def turn_left(i, _):
        for x in range(4):
            share_arrival(lbuf.at[4 * i + x], l_recv.at[4 * i + x])
        flipped = [lbuf[4 * i + x].astype(F32).T for x in range(4)]
        for x in range(4):
            for part in range(kp // 128):
                lturn[part, pl.ds(4 * i + x, all_c, stride=n), :] = flipped[x][
                    :, part * 128:(part + 1) * 128
                ]
        return 0

    lax.fori_loop(0, n // 4, turn_left, 0)

    def pack_left(i, _):
        rows = pl.ds(pl.multiple_of(i * 128, 128), 128)
        for part in range(kp // 128):
            lrows[rows, part * 128:(part + 1) * 128] = lturn[part, rows, :].astype(BF16)
        return 0

    lax.fori_loop(0, all_c * n // 128, pack_left, 0)

    c_step = ybuf.shape[2] // width
    rows_c = c_step * n
    block_rows = slots * n
    early = ybuf.shape[0] > 1

    def take_amps():
        for e in range(row_n):
            for i in range(pairs_of_cols):
                r, c = (row + e) % row_n, 2 * ((cpair + i) % pairs_of_cols) + 1 - half
                arrival(t_block(r, c), t_recv.at[r * col_n + c])

        def turn_amps(i, _):
            for h in range(4):
                at = pl.multiple_of((4 * i + h) * width, width)
                tturn[pl.ds(at, width), :] = tbuf[4 * i + h].astype(F32).T.astype(BF16)
            return 0

        if early:
            lax.fori_loop(0, all_c // 4, turn_amps, 0)

    def s1_copy(step, e):
        r, k, slot = (row + e) % row_n, phase(step), step % 2
        return pltpu.make_async_remote_copy(
            src_ref=out1.at[slot, r], dst_ref=in1.at[k, row],
            send_sem=s1_send.at[slot * row_n + r], recv_sem=s1_recv.at[k * row_n + row],
            device_id=(r, col), device_id_type=MESH,
        )

    def land(step):
        k = phase(step)
        source = 2 * ((cpair + k) % pairs_of_cols)

        def landed(j, _):
            s = (j // 2) * col_n + source + j % 2
            share_arrival(rbuf.at[k, j], r_recv.at[s])
            return 0

        lax.fori_loop(0, slots, landed, 0)

    def integrals(step, ci, lead, first_row):
        k = phase(step)
        at = pl.multiple_of(ci * rows_c, rows_c)

        def some_b(j, _):
            weights = jnp.concatenate([rbuf[k, 2 * j], rbuf[k, 2 * j + 1]], axis=1)
            block = jnp.dot(
                lrows[pl.ds(at, rows_c), :], weights, preferred_element_type=F32
            ).astype(BF16).reshape(c_step, n, 2 * width)
            for x in range(2):
                spot = pl.ds(pl.multiple_of(first_row + (2 * j + x) * n, n), n)
                for c in range(c_step):
                    ybuf[lead, spot, c * width:(c + 1) * width] = block[
                        c, :, x * width:(x + 1) * width
                    ]
            return 0

        lax.fori_loop(0, row_n, some_b, 0)

    def emit(step, first_row):
        @pl.when(step >= 2)
        def _():
            for e in range(1, row_n):
                s1_copy(step, e).wait_send()

        part = acc[pl.ds(first_row, block_rows), :].reshape(slots, row_n, a_own, all_p)
        for r in range(row_n):
            out1[step % 2, r] = part[:, r]
        for e in range(1, row_n):
            s1_copy(step, e).start()
        in1[phase(step), row] = out1[step % 2, row]

    def all_integrals(step, _):
        land(step)
        first_row = pl.multiple_of(step * block_rows, block_rows)

        def some_c(ci, _):
            integrals(step, ci, ci, first_row)
            return 0

        lax.fori_loop(0, all_c // c_step, some_c, 0)
        return 0

    def ladder(first_row, rows):
        acc[pl.ds(0, rows), :] = jnp.zeros((rows, all_p), F32)

        def some_c(ci, _):
            depth = c_step * width
            at = pl.multiple_of(ci * depth, depth)
            acc[pl.ds(0, rows), :] += jnp.dot(
                ybuf[ci, pl.ds(first_row, rows), :], tturn[pl.ds(at, depth), :],
                preferred_element_type=F32,
            )
            return 0

        lax.fori_loop(0, all_c // c_step, some_c, 0)

    def chunk(step, _):
        land(step)
        acc[...] = jnp.zeros_like(acc)

        def some_c(ci, _):
            integrals(step, ci, 0, 0)
            amp = jnp.concatenate([tbuf[c_step * ci + c] for c in range(c_step)], axis=1)
            acc[...] += lax.dot_general(
                ybuf[0], amp, (((1,), (1,)), ((), ())), preferred_element_type=F32
            )
            return 0

        lax.fori_loop(0, all_c // c_step, some_c, 0)
        emit(step, 0)
        return 0

    if early:
        lax.fori_loop(0, 2, all_integrals, 0)
        take_amps()
        ladder(0, 2 * block_rows)
        for step in range(2):
            emit(step, step * block_rows)

        def later(step, _):
            all_integrals(step, 0)
            ladder(pl.multiple_of(step * block_rows, block_rows), block_rows)
            emit(step, 0)
            return 0

        lax.fori_loop(2, pairs_of_cols, later, 0)
    else:
        take_amps()
        lax.fori_loop(0, pairs_of_cols, chunk, 0)

    def gather_rows(step, _):
        k = phase(step)
        part = in1[k, row]
        for e in range(1, row_n):
            r = (row + e) % row_n
            arrival(in1.at[k, r], s1_recv.at[k * row_n + r])
            part += in1[k, r]
        source = 2 * ((cpair + k) % pairs_of_cols)
        for j in range(slots):
            b = (j // 2) * col_n + source + j % 2
            for x in range(all_p // 128):
                fin[x, pl.ds(b, a_own, stride=n), :] = part[j, :, x * 128:(x + 1) * 128]
        return 0

    lax.fori_loop(0, pairs_of_cols, gather_rows, 0)
    for x in range(all_p // 128):
        out2[x * 128:(x + 1) * 128, :] = fin[x].T

    def s2_copy(e):
        c = (col + e) % col_n
        return pltpu.make_async_remote_copy(
            src_ref=out2.at[pl.ds(c * pb, pb), :], dst_ref=in2.at[col],
            send_sem=s2_send.at[c], recv_sem=s2_recv.at[col],
            device_id=(row, c), device_id_type=MESH,
        )

    for e in range(1, col_n):
        s2_copy(e).start()
    total = out2[pl.ds(pl.multiple_of(col * pb, pb), pb), :]
    for e in range(1, col_n):
        c = (col + e) % col_n
        arrival(in2.at[c], s2_recv.at[c])
        total += in2[c]
    out[...] = (total / den[...]).astype(out.dtype)

    for i in range(len(hops)):
        t1_copy(i).wait_send()
    for i in range(pairs_of_cols):
        for e in range(row_n):
            if e > 0:
                t2_copy(i, e).wait_send()
            t3_copy(i, e).wait_send()

    for step in range(max(0, pairs_of_cols - 2), pairs_of_cols):
        for e in range(1, row_n):
            s1_copy(step, e).wait_send()

    def drain(e, _):
        d = (me + e) % n
        left_share(d, begun)
        right_share(0, d, begun)
        return 0

    lax.fori_loop(1, n, drain, 0)
    for e in range(1, col_n):
        s2_copy(e).wait_send()


def shards(panel_left, panel_right, amplitudes, eps_virtual, eps_occupied, pair_list, blocks):
    row_n = lax.axis_size("row")
    col_n = lax.axis_size("col")
    n = row_n * col_n
    fit, _, width = panel_left.shape
    pb, cb, _ = amplitudes.shape
    units = -(-fit // 16)
    base, extra = units // n, units % n
    kp = -(-16 * (base + 1) // 128) * 128
    left = panel_left.reshape(fit, width)
    right = panel_right.reshape(fit, width)
    last = 16 * (units - 1)
    tails = jnp.pad(jnp.stack([left[last:], right[last:]]), ((0, 0), (0, 16 * units - fit), (0, 0)))
    amps = jnp.transpose(amplitudes, (1, 0, 2))
    all_c, all_p = cb * row_n, pb * col_n
    halves = col_n // 2
    slots = 2 * row_n
    a_own = n // row_n
    span = n * a_own
    early = all_c * n * n * width <= 2 ** 24 and all_p <= width
    c_step = 32 if early else 2
    dma = pltpu.SemaphoreType.DMA
    hbm = pl.BlockSpec(memory_space=pl.ANY)
    smem = pl.BlockSpec(memory_space=pltpu.SMEM)
    flat = pl.pallas_call(
        functools.partial(kernel, row_n, col_n, base, extra),
        out_shape=jax.ShapeDtypeStruct((pb, span), BF16),
        in_specs=[hbm, hbm, hbm, hbm, smem, smem, smem, smem],
        out_specs=pl.BlockSpec(memory_space=pltpu.VMEM),
        scratch_shapes=[
            pltpu.VMEM((n, kp, width), BF16),
            pltpu.VMEM((halves, slots, kp, width), BF16),
            pltpu.VMEM((kp // 128, all_c * n, 128), F32),
            pltpu.VMEM((all_c * n, kp), BF16),
            pltpu.VMEM((all_c, all_p, width), BF16),
            pltpu.VMEM((all_c * width if early else 16, all_p), BF16),
            pltpu.VMEM(
                (all_c // c_step, n * n, c_step * width) if early else (1, slots * n, c_step * width),
                BF16,
            ),
            pltpu.VMEM((2 * slots * n if early else slots * n, all_p), F32),
            pltpu.VMEM((2, row_n, slots, a_own, all_p), F32),
            pltpu.VMEM((halves, row_n, slots, a_own, all_p), F32),
            pltpu.VMEM((all_p // 128, span, 128), F32),
            pltpu.VMEM((all_p, span), F32),
            pltpu.VMEM((col_n, pb, span), F32),
            pltpu.VMEM((pb, span), F32),
            dma((n,)), dma((n,)), dma((n,)), dma((n,)),
            dma((halves,)), dma((halves * row_n,)), dma((halves * row_n,)), dma((n,)),
            dma((2 * row_n,)), dma((halves * row_n,)), dma((col_n,)), dma((col_n,)),
        ],
        compiler_params=pltpu.CompilerParams(
            collective_id=0, has_side_effects=True, vmem_limit_bytes=62 * 1024 * 1024
        ),
        cost_estimate=pl.CostEstimate(
            flops=2 * fit * width * width * n, bytes_accessed=4 * fit * width, transcendentals=0
        ),
        name="ladder_exchange",
    )(left, right, tails, amps, eps_virtual, eps_occupied, pair_list.T, blocks)
    return flat.reshape(pb, a_own, n)


def solution(mesh):
    return jax.shard_map(
        shards,
        mesh=mesh,
        in_specs=(
            P(None, ("row", "col"), None),
            P(None, ("row", "col"), None),
            P("col", "row", None),
            P(),
            P(),
            P(),
            P(),
        ),
        out_specs=P("col", "row", None),
        check_vma=False,
    )
```

```python
import functools

import jax
import jax.numpy as jnp
from jax import lax
from jax.experimental import pallas as pl
from jax.experimental.pallas import tpu as pltpu
from jax.sharding import PartitionSpec as P

MESH = pl.DeviceIdType.MESH
F32 = jnp.float32
BF16 = jnp.bfloat16


def arrival(ref, sem):
    pltpu.make_async_copy(ref, ref, sem).wait()


def kernel(
    row_n, col_n, base, extra,
    left, right, tails, amps, eps_v, eps_o, pairs, blocks,
    out,
    lbuf, rbuf, lturn, lrows, tbuf, tturn, ybuf, acc, out1, in1, fin, out2, in2, den,
    l_send, l_recv, r_send, r_recv, t_send1, t_send2, t_send3, t_recv,
    s1_send, s1_recv, s2_send, s2_recv,
):
    n = row_n * col_n
    pairs_of_cols = col_n // 2
    slots = 2 * row_n
    cb, pb, width = amps.shape
    all_c = cb * row_n
    all_p = pb * col_n
    kp = lbuf.shape[1]
    few, most = 16 * base, 16 * (base + 1)
    a_own = n // row_n
    row = lax.axis_index("row")
    col = lax.axis_index("col")
    me = row * col_n + col
    cpair = col // 2
    half = col % 2

    barrier = pltpu.get_barrier_semaphore()

    def greet(e, _):
        d = (me + e) % n
        pl.semaphore_signal(barrier, inc=1, device_id=(d // col_n, d % col_n), device_id_type=MESH)
        return 0

    lax.fori_loop(1, n, greet, 0)

    def t_block(r, c):
        return tbuf.at[pl.ds(r * cb, cb), pl.ds(c * pb, pb), :]

    pltpu.make_async_copy(amps, t_block(row, col), t_recv.at[me]).start()

    def shares(src, which, dst, d, copy, act):
        @pl.when(d < extra)
        def _():
            act(copy(src.at[pl.ds(d * most, most), :], dst.at[pl.ds(0, most), :]))

        @pl.when((d >= extra) & (d < n - 1))
        def _():
            at = extra * most + (d - extra) * few
            act(copy(src.at[pl.ds(at, few), :], dst.at[pl.ds(0, few), :]))

        @pl.when(d == n - 1)
        def _():
            at = extra * most + (n - 1 - extra) * few
            act(copy(src.at[pl.ds(at, few - 16), :], dst.at[pl.ds(0, few - 16), :]))
            act(copy(tails.at[which], dst.at[pl.ds(few - 16, 16), :]))

    def share_arrival(ref, sem):
        @pl.when(me < extra)
        def _():
            arrival(ref.at[pl.ds(0, most), :], sem)

        @pl.when(me >= extra)
        def _():
            arrival(ref.at[pl.ds(0, few), :], sem)

    def begin(copy):
        copy.start()

    def begun(copy):
        copy.wait_send()

    shares(left, 0, lbuf.at[me], me, lambda a, b: pltpu.make_async_copy(a, b, l_recv.at[me]), begin)
    shares(
        right, 1, rbuf.at[0, row * 2 + half], me,
        lambda a, b: pltpu.make_async_copy(a, b, r_recv.at[me]), begin,
    )

    def clear(at):
        def one(i, _):
            lbuf[i, pl.ds(at, kp - at), :] = jnp.zeros((kp - at, width), BF16)
            rbuf[i // slots, i % slots, pl.ds(at, kp - at), :] = jnp.zeros((kp - at, width), BF16)
            return 0

        lax.fori_loop(0, n, one, 0)

    if kp > most:
        @pl.when(me < extra)
        def _():
            clear(most)

    @pl.when(me >= extra)
    def _():
        clear(few)

    pl.semaphore_wait(barrier, n - 1)

    def mate(i):
        other, bit = cpair, 1
        while bit <= i:
            if i & bit:
                other = other + bit * (1 - 2 * ((other // bit) % 2))
            bit *= 2
        return 2 * other + half

    hops, bit, held = [], pairs_of_cols // 2, [0]
    while bit:
        hops += [(block, bit) for block in held]
        held += [block + bit for block in held]
        bit //= 2

    def t1_copy(i):
        block, partner = hops[i]
        c = mate(block)
        return pltpu.make_async_remote_copy(
            src_ref=t_block(row, c), dst_ref=t_block(row, c),
            send_sem=t_send1.at[i], recv_sem=t_recv.at[row * col_n + c],
            device_id=(row, mate(partner)), device_id_type=MESH,
        )

    def t2_copy(i, e):
        c = mate(i)
        return pltpu.make_async_remote_copy(
            src_ref=t_block(row, c), dst_ref=t_block(row, c),
            send_sem=t_send2.at[i * row_n + e], recv_sem=t_recv.at[row * col_n + c],
            device_id=((row + e) % row_n, col), device_id_type=MESH,
        )

    def t3_copy(i, e):
        c, r = mate(i), (row + e) % row_n
        return pltpu.make_async_remote_copy(
            src_ref=t_block(r, c), dst_ref=t_block(r, c),
            send_sem=t_send3.at[i * row_n + e], recv_sem=t_recv.at[r * col_n + c],
            device_id=(row, 2 * cpair + 1 - half), device_id_type=MESH,
        )

    def target(k, j):
        spot = (row * 2 + half + j) % slots
        return (spot // 2) * col_n + 2 * ((cpair + pairs_of_cols - k) % pairs_of_cols) + spot % 2

    def remote(send, recv, d):
        return lambda a, b: pltpu.make_async_remote_copy(
            src_ref=a, dst_ref=b, send_sem=send.at[d], recv_sem=recv.at[me],
            device_id=(d // col_n, d % col_n), device_id_type=MESH,
        )

    def left_share(d, act):
        shares(left, 0, lbuf.at[me], d, remote(l_send, l_recv, d), act)

    def right_share(k, d, act):
        shares(right, 1, rbuf.at[k, row * 2 + half], d, remote(r_send, r_recv, d), act)

    def phase(step):
        return ((step + pairs_of_cols - 1) // pairs_of_cols) * (1 + step % (pairs_of_cols - 1))

    def send_left(j, _):
        def one(step, _):
            d = target(phase((step + 1) % pairs_of_cols), j)

            @pl.when(d != me)
            def _():
                left_share(d, begin)

            return 0

        lax.fori_loop(0, pairs_of_cols, one, 0)
        return 0

    def send_right(first, count, start, stop):
        def one(i, _):
            k = phase(first + i % count)
            d = target(k, i // count)

            @pl.when(d != me)
            def _():
                right_share(k, d, begin)

            return 0

        lax.fori_loop(count * start, count * stop, one, 0)

    here = set()

    def need(block):
        if block not in here:
            here.add(block)
            c = mate(block)
            arrival(t_block(row, c), t_recv.at[row * col_n + c])

    for own in (True, False):
        for i, (block, _) in enumerate(hops):
            if (block == 0) == own:
                need(block)
                t1_copy(i).start()
        lax.fori_loop(0 if own else slots // 4, slots // 4 if own else slots, send_left, 0)
    for i in range(pairs_of_cols):
        need(i)
        for e in range(1, row_n):
            t2_copy(i, e).start()
        t3_copy(i, 0).start()
        send_right(0, 2, i * slots // pairs_of_cols, (i + 1) * slots // pairs_of_cols)
    for step in range(2, pairs_of_cols - 1):
        send_right(step, 1, 0, slots)

    span = n * a_own
    lane = lax.broadcasted_iota(jnp.int32, (pb, span), 1)
    line = lax.broadcasted_iota(jnp.int32, (pb, span), 0)
    first_at = blocks[0] * n + row * a_own
    second_at = blocks[1] * n
    first = jnp.zeros((pb, span), F32)
    for i in range(a_own):
        first = jnp.where(lane // n == i, eps_v[first_at + i], first)
    den[...] = first

    def add_second(b, _):
        den[...] = jnp.where(lane % n == b, den[...] + eps_v[second_at + b], den[...])
        return 0

    lax.fori_loop(0, n, add_second, 0)
    pair_sum = jnp.zeros((pb, span), F32)
    for i in range(pb):
        at = col * pb + i
        level = eps_o[pairs[0, at]] + eps_o[pairs[1, at]]
        pair_sum = jnp.where(line == i, level, pair_sum)
    den[...] = den[...] - pair_sum

    spans = [(lo, min(lo + 128, most)) for lo in range(0, kp, 128)]

    def turn_left(i, _):
        for x in range(4):
            share_arrival(lbuf.at[4 * i + x], l_recv.at[4 * i + x])
        flipped = [
            [lbuf[4 * i + x, lo:hi, :].astype(F32).T for lo, hi in spans] for x in range(4)
        ]
        for x in range(4):
            for part, (lo, hi) in enumerate(spans):
                lturn[part, pl.ds(4 * i + x, all_c, stride=n), :hi - lo] = flipped[x][part]
        return 0

    lax.fori_loop(0, n // 4, turn_left, 0)

    def pack_left(i, _):
        rows = pl.ds(pl.multiple_of(i * 128, 128), 128)
        for part in range(kp // 128):
            lo, hi = spans[part]
            turned = lturn[part, rows, :]
            if hi - lo < 128:
                spot = lax.broadcasted_iota(jnp.int32, turned.shape, 1)
                turned = jnp.where(spot < hi - lo, turned, 0.0)
            lrows[rows, lo:lo + 128] = turned.astype(BF16)
        return 0

    lax.fori_loop(0, all_c * n // 128, pack_left, 0)

    for e in range(1, row_n):
        for i in range(pairs_of_cols):
            r, c = (row + e) % row_n, mate(i)
            arrival(t_block(r, c), t_recv.at[r * col_n + c])
            t3_copy(i, e).start()
    if pairs_of_cols > 2:
        send_right(pairs_of_cols - 1, 1, 0, slots)

    c_step = ybuf.shape[2] // width
    rows_c = c_step * n
    block_rows = slots * n
    early = ybuf.shape[0] > 1

    def take_amps():
        for e in range(row_n):
            for i in range(pairs_of_cols):
                r, c = (row + e) % row_n, 2 * ((cpair + i) % pairs_of_cols) + 1 - half
                arrival(t_block(r, c), t_recv.at[r * col_n + c])

        def turn_amps(i, _):
            for h in range(4):
                at = pl.multiple_of((4 * i + h) * width, width)
                tturn[pl.ds(at, width), :] = tbuf[4 * i + h].astype(F32).T.astype(BF16)
            return 0

        if early:
            lax.fori_loop(0, all_c // 4, turn_amps, 0)

    def s1_copy(step, e):
        r, k, slot = (row + e) % row_n, phase(step), step % 2
        return pltpu.make_async_remote_copy(
            src_ref=out1.at[slot, r], dst_ref=in1.at[k, row],
            send_sem=s1_send.at[slot * row_n + r], recv_sem=s1_recv.at[k * row_n + row],
            device_id=(r, col), device_id_type=MESH,
        )

    def land(step):
        k = phase(step)
        source = 2 * ((cpair + k) % pairs_of_cols)

        def landed(j, _):
            s = (j // 2) * col_n + source + j % 2
            share_arrival(rbuf.at[k, j], r_recv.at[s])
            return 0

        lax.fori_loop(0, slots, landed, 0)

    def integrals(step, ci, lead, first_row):
        k = phase(step)
        at = pl.multiple_of(ci * rows_c, rows_c)

        def some_b(j, _):
            weights = jnp.concatenate([rbuf[k, 2 * j], rbuf[k, 2 * j + 1]], axis=1)
            block = jnp.dot(
                lrows[pl.ds(at, rows_c), :], weights, preferred_element_type=F32
            ).astype(BF16).reshape(c_step, n, 2 * width)
            for x in range(2):
                spot = pl.ds(pl.multiple_of(first_row + (2 * j + x) * n, n), n)
                for c in range(c_step):
                    ybuf[lead, spot, c * width:(c + 1) * width] = block[
                        c, :, x * width:(x + 1) * width
                    ]
            return 0

        lax.fori_loop(0, row_n, some_b, 0)

    def emit(step, first_row):
        @pl.when(step >= 2)
        def _():
            for e in range(1, row_n):
                s1_copy(step, e).wait_send()

        part = acc[pl.ds(first_row, block_rows), :].reshape(slots, row_n, a_own, all_p)
        for r in range(row_n):
            out1[step % 2, r] = part[:, r]
        for e in range(1, row_n):
            s1_copy(step, e).start()
        in1[phase(step), row] = out1[step % 2, row]

    def all_integrals(step, _):
        land(step)
        first_row = pl.multiple_of(step * block_rows, block_rows)

        def some_c(ci, _):
            integrals(step, ci, ci, first_row)
            return 0

        lax.fori_loop(0, all_c // c_step, some_c, 0)
        return 0

    def ladder(first_row, rows):
        acc[pl.ds(0, rows), :] = jnp.zeros((rows, all_p), F32)

        def some_c(ci, _):
            depth = c_step * width
            at = pl.multiple_of(ci * depth, depth)
            acc[pl.ds(0, rows), :] += jnp.dot(
                ybuf[ci, pl.ds(first_row, rows), :], tturn[pl.ds(at, depth), :],
                preferred_element_type=F32,
            )
            return 0

        lax.fori_loop(0, all_c // c_step, some_c, 0)

    def chunk(step, _):
        land(step)
        acc[...] = jnp.zeros_like(acc)

        def some_c(ci, _):
            integrals(step, ci, 0, 0)
            amp = jnp.concatenate([tbuf[c_step * ci + c] for c in range(c_step)], axis=1)
            acc[...] += lax.dot_general(
                ybuf[0], amp, (((1,), (1,)), ((), ())), preferred_element_type=F32
            )
            return 0

        lax.fori_loop(0, all_c // c_step, some_c, 0)
        emit(step, 0)
        return 0

    if early:
        lax.fori_loop(0, 2, all_integrals, 0)
        take_amps()
        ladder(0, 2 * block_rows)
        for step in range(2):
            emit(step, step * block_rows)

        def later(step, _):
            all_integrals(step, 0)
            ladder(pl.multiple_of(step * block_rows, block_rows), block_rows)
            emit(step, 0)
            return 0

        lax.fori_loop(2, pairs_of_cols, later, 0)
    else:
        take_amps()
        lax.fori_loop(0, pairs_of_cols, chunk, 0)

    def gather_rows(step, _):
        k = phase(step)
        part = in1[k, row]
        for e in range(1, row_n):
            r = (row + e) % row_n
            arrival(in1.at[k, r], s1_recv.at[k * row_n + r])
            part += in1[k, r]
        source = 2 * ((cpair + k) % pairs_of_cols)
        for j in range(slots):
            b = (j // 2) * col_n + source + j % 2
            for x in range(all_p // 128):
                fin[x, pl.ds(b, a_own, stride=n), :] = part[j, :, x * 128:(x + 1) * 128]
        return 0

    lax.fori_loop(0, pairs_of_cols, gather_rows, 0)
    for x in range(all_p // 128):
        out2[x * 128:(x + 1) * 128, :] = fin[x].T

    def s2_copy(e):
        c = (col + e) % col_n
        return pltpu.make_async_remote_copy(
            src_ref=out2.at[pl.ds(c * pb, pb), :], dst_ref=in2.at[col],
            send_sem=s2_send.at[c], recv_sem=s2_recv.at[col],
            device_id=(row, c), device_id_type=MESH,
        )

    for e in range(1, col_n):
        s2_copy(e).start()
    total = out2[pl.ds(pl.multiple_of(col * pb, pb), pb), :]
    for e in range(1, col_n):
        c = (col + e) % col_n
        arrival(in2.at[c], s2_recv.at[c])
        total += in2[c]
    out[...] = (total / den[...]).astype(out.dtype)

    for i in range(len(hops)):
        t1_copy(i).wait_send()
    for i in range(pairs_of_cols):
        for e in range(row_n):
            if e > 0:
                t2_copy(i, e).wait_send()
            t3_copy(i, e).wait_send()

    for step in range(max(0, pairs_of_cols - 2), pairs_of_cols):
        for e in range(1, row_n):
            s1_copy(step, e).wait_send()

    def drain(e, _):
        d = (me + e) % n
        left_share(d, begun)
        right_share(0, d, begun)
        return 0

    lax.fori_loop(1, n, drain, 0)
    for e in range(1, col_n):
        s2_copy(e).wait_send()


def shards(panel_left, panel_right, amplitudes, eps_virtual, eps_occupied, pair_list, blocks):
    row_n = lax.axis_size("row")
    col_n = lax.axis_size("col")
    n = row_n * col_n
    fit, _, width = panel_left.shape
    pb, cb, _ = amplitudes.shape
    units = -(-fit // 16)
    base, extra = units // n, units % n
    kp = -(-16 * (base + 1) // 128) * 128
    left = panel_left.reshape(fit, width)
    right = panel_right.reshape(fit, width)
    last = 16 * (units - 1)
    tails = jnp.pad(jnp.stack([left[last:], right[last:]]), ((0, 0), (0, 16 * units - fit), (0, 0)))
    amps = jnp.transpose(amplitudes, (1, 0, 2))
    all_c, all_p = cb * row_n, pb * col_n
    halves = col_n // 2
    slots = 2 * row_n
    a_own = n // row_n
    span = n * a_own
    early = all_c * n * n * width <= 2 ** 24 and all_p <= width
    c_step = 32 if early else 2
    dma = pltpu.SemaphoreType.DMA
    hbm = pl.BlockSpec(memory_space=pl.ANY)
    smem = pl.BlockSpec(memory_space=pltpu.SMEM)
    flat = pl.pallas_call(
        functools.partial(kernel, row_n, col_n, base, extra),
        out_shape=jax.ShapeDtypeStruct((pb, span), BF16),
        in_specs=[hbm, hbm, hbm, hbm, smem, smem, smem, smem],
        out_specs=pl.BlockSpec(memory_space=pltpu.VMEM),
        scratch_shapes=[
            pltpu.VMEM((n, kp, width), BF16),
            pltpu.VMEM((halves, slots, kp, width), BF16),
            pltpu.VMEM((kp // 128, all_c * n, 128), F32),
            pltpu.VMEM((all_c * n, kp), BF16),
            pltpu.VMEM((all_c, all_p, width), BF16),
            pltpu.VMEM((all_c * width if early else 16, all_p), BF16),
            pltpu.VMEM(
                (all_c // c_step, n * n, c_step * width) if early else (1, slots * n, c_step * width),
                BF16,
            ),
            pltpu.VMEM((2 * slots * n if early else slots * n, all_p), F32),
            pltpu.VMEM((2, row_n, slots, a_own, all_p), F32),
            pltpu.VMEM((halves, row_n, slots, a_own, all_p), F32),
            pltpu.VMEM((all_p // 128, span, 128), F32),
            pltpu.VMEM((all_p, span), F32),
            pltpu.VMEM((col_n, pb, span), F32),
            pltpu.VMEM((pb, span), F32),
            dma((n,)), dma((n,)), dma((n,)), dma((n,)),
            dma((halves,)), dma((halves * row_n,)), dma((halves * row_n,)), dma((n,)),
            dma((2 * row_n,)), dma((halves * row_n,)), dma((col_n,)), dma((col_n,)),
        ],
        compiler_params=pltpu.CompilerParams(
            collective_id=0, has_side_effects=True, vmem_limit_bytes=62 * 1024 * 1024
        ),
        cost_estimate=pl.CostEstimate(
            flops=2 * fit * width * width * n, bytes_accessed=4 * fit * width, transcendentals=0
        ),
        name="ladder_exchange",
    )(left, right, tails, amps, eps_virtual, eps_occupied, pair_list.T, blocks)
    return flat.reshape(pb, a_own, n)


def solution(mesh):
    return jax.shard_map(
        shards,
        mesh=mesh,
        in_specs=(
            P(None, ("row", "col"), None),
            P(None, ("row", "col"), None),
            P("col", "row", None),
            P(),
            P(),
            P(),
            P(),
        ),
        out_specs=P("col", "row", None),
        check_vma=False,
    )
```

```python
import functools

import jax
import jax.numpy as jnp
from jax import lax
from jax.experimental import pallas as pl
from jax.experimental.pallas import tpu as pltpu
from jax.sharding import PartitionSpec as P

MESH = pl.DeviceIdType.MESH
F32 = jnp.float32
BF16 = jnp.bfloat16


def arrival(ref, sem):
    pltpu.make_async_copy(ref, ref, sem).wait()


def kernel(
    row_n, col_n, base, extra,
    left, right, tails, amps, eps_v, eps_o, pairs, blocks,
    out,
    lbuf, rbuf, lturn, lrows, tbuf, tturn, ybuf, acc, out1, in1, fin, out2, in2, den,
    l_send, l_recv, r_send, r_recv, t_send1, t_send2, t_send3, t_recv,
    s1_send, s1_recv, s2_send, s2_recv,
):
    n = row_n * col_n
    pairs_of_cols = col_n // 2
    slots = 2 * row_n
    cb, pb, width = amps.shape
    all_c = cb * row_n
    all_p = pb * col_n
    kp = lbuf.shape[1]
    few, most = 16 * base, 16 * (base + 1)
    a_own = n // row_n
    row = lax.axis_index("row")
    col = lax.axis_index("col")
    me = row * col_n + col
    cpair = col // 2
    half = col % 2

    barrier = pltpu.get_barrier_semaphore()

    def greet(e, _):
        d = (me + e) % n
        pl.semaphore_signal(barrier, inc=1, device_id=(d // col_n, d % col_n), device_id_type=MESH)
        return 0

    lax.fori_loop(1, n, greet, 0)

    def t_block(r, c):
        return tbuf.at[pl.ds(r * cb, cb), pl.ds(c * pb, pb), :]

    pltpu.make_async_copy(amps, t_block(row, col), t_recv.at[me]).start()

    def shares(src, which, dst, d, copy, act):
        @pl.when(d < extra)
        def _():
            act(copy(src.at[pl.ds(d * most, most), :], dst.at[pl.ds(0, most), :]))

        @pl.when((d >= extra) & (d < n - 1))
        def _():
            at = extra * most + (d - extra) * few
            act(copy(src.at[pl.ds(at, few), :], dst.at[pl.ds(0, few), :]))

        @pl.when(d == n - 1)
        def _():
            at = extra * most + (n - 1 - extra) * few
            act(copy(src.at[pl.ds(at, few - 16), :], dst.at[pl.ds(0, few - 16), :]))
            act(copy(tails.at[which], dst.at[pl.ds(few - 16, 16), :]))

    def share_arrival(ref, sem):
        @pl.when(me < extra)
        def _():
            arrival(ref.at[pl.ds(0, most), :], sem)

        @pl.when(me >= extra)
        def _():
            arrival(ref.at[pl.ds(0, few), :], sem)

    def begin(copy):
        copy.start()

    def begun(copy):
        copy.wait_send()

    shares(left, 0, lbuf.at[me], me, lambda a, b: pltpu.make_async_copy(a, b, l_recv.at[me]), begin)
    shares(
        right, 1, rbuf.at[0, row * 2 + half], me,
        lambda a, b: pltpu.make_async_copy(a, b, r_recv.at[me]), begin,
    )

    def clear(at):
        def one(i, _):
            lbuf[i, pl.ds(at, kp - at), :] = jnp.zeros((kp - at, width), BF16)
            rbuf[i // slots, i % slots, pl.ds(at, kp - at), :] = jnp.zeros((kp - at, width), BF16)
            return 0

        lax.fori_loop(0, n, one, 0)

    if kp > most:
        @pl.when(me < extra)
        def _():
            clear(most)

    @pl.when(me >= extra)
    def _():
        clear(few)

    pl.semaphore_wait(barrier, n - 1)

    def mate(i):
        other, bit = cpair, 1
        while bit <= i:
            if i & bit:
                other = other + bit * (1 - 2 * ((other // bit) % 2))
            bit *= 2
        return 2 * other + half

    hops, bit, held = [], pairs_of_cols // 2, [0]
    while bit:
        hops += [(block, bit) for block in held]
        held += [block + bit for block in held]
        bit //= 2

    def t1_copy(i):
        block, partner = hops[i]
        c = mate(block)
        return pltpu.make_async_remote_copy(
            src_ref=t_block(row, c), dst_ref=t_block(row, c),
            send_sem=t_send1.at[i], recv_sem=t_recv.at[row * col_n + c],
            device_id=(row, mate(partner)), device_id_type=MESH,
        )

    def t2_copy(i, e):
        c = mate(i)
        return pltpu.make_async_remote_copy(
            src_ref=t_block(row, c), dst_ref=t_block(row, c),
            send_sem=t_send2.at[i * row_n + e], recv_sem=t_recv.at[row * col_n + c],
            device_id=((row + e) % row_n, col), device_id_type=MESH,
        )

    def t3_copy(i, e):
        c, r = mate(i), (row + e) % row_n
        return pltpu.make_async_remote_copy(
            src_ref=t_block(r, c), dst_ref=t_block(r, c),
            send_sem=t_send3.at[i * row_n + e], recv_sem=t_recv.at[r * col_n + c],
            device_id=(row, 2 * cpair + 1 - half), device_id_type=MESH,
        )

    def target(k, j):
        to_row, to_half = (row + j // 2) % row_n, (half + j) % 2
        return to_row * col_n + 2 * ((cpair + pairs_of_cols - k) % pairs_of_cols) + to_half

    def remote(send, recv, d):
        return lambda a, b: pltpu.make_async_remote_copy(
            src_ref=a, dst_ref=b, send_sem=send.at[d], recv_sem=recv.at[me],
            device_id=(d // col_n, d % col_n), device_id_type=MESH,
        )

    def left_share(d, act):
        shares(left, 0, lbuf.at[me], d, remote(l_send, l_recv, d), act)

    def right_share(k, d, act):
        shares(right, 1, rbuf.at[k, row * 2 + half], d, remote(r_send, r_recv, d), act)

    def phase(step):
        return ((step + pairs_of_cols - 1) // pairs_of_cols) * (1 + step % (pairs_of_cols - 1))

    def send_left(j, _):
        def one(step, _):
            d = target(phase((step + 1) % pairs_of_cols), j)

            @pl.when(d != me)
            def _():
                left_share(d, begin)

            return 0

        lax.fori_loop(0, pairs_of_cols, one, 0)
        return 0

    def send_right(first, count, start, stop):
        def one(i, _):
            k = phase(first + i % count)
            d = target(k, i // count)

            @pl.when(d != me)
            def _():
                right_share(k, d, begin)

            return 0

        lax.fori_loop(count * start, count * stop, one, 0)

    here = set()

    def need(block):
        if block not in here:
            here.add(block)
            c = mate(block)
            arrival(t_block(row, c), t_recv.at[row * col_n + c])

    for own in (True, False):
        for i, (block, _) in enumerate(hops):
            if (block == 0) == own:
                need(block)
                t1_copy(i).start()
        lax.fori_loop(0 if own else slots // 4, slots // 4 if own else slots, send_left, 0)
    for i in range(pairs_of_cols):
        need(i)
        for e in range(1, row_n):
            t2_copy(i, e).start()
        t3_copy(i, 0).start()
        send_right(0, 2, i * slots // pairs_of_cols, (i + 1) * slots // pairs_of_cols)
    for step in range(2, pairs_of_cols):
        send_right(step, 1, 0, slots)

    span = n * a_own
    lane = lax.broadcasted_iota(jnp.int32, (pb, span), 1)
    line = lax.broadcasted_iota(jnp.int32, (pb, span), 0)
    first_at = blocks[0] * n + row * a_own
    second_at = blocks[1] * n
    first = jnp.zeros((pb, span), F32)
    for i in range(a_own):
        first = jnp.where(lane // n == i, eps_v[first_at + i], first)
    den[...] = first

    def add_second(b, _):
        den[...] = jnp.where(lane % n == b, den[...] + eps_v[second_at + b], den[...])
        return 0

    lax.fori_loop(0, n, add_second, 0)
    pair_sum = jnp.zeros((pb, span), F32)
    for i in range(pb):
        at = col * pb + i
        level = eps_o[pairs[0, at]] + eps_o[pairs[1, at]]
        pair_sum = jnp.where(line == i, level, pair_sum)
    den[...] = den[...] - pair_sum

    spans = [(lo, min(lo + 128, most)) for lo in range(0, kp, 128)]

    def turn_left(i, _):
        for x in range(4):
            share_arrival(lbuf.at[4 * i + x], l_recv.at[4 * i + x])
        flipped = [
            [lbuf[4 * i + x, lo:hi, :].astype(F32).T for lo, hi in spans] for x in range(4)
        ]
        for x in range(4):
            for part, (lo, hi) in enumerate(spans):
                lturn[part, pl.ds(4 * i + x, all_c, stride=n), :hi - lo] = flipped[x][part]
        return 0

    lax.fori_loop(0, n // 4, turn_left, 0)

    def pack_left(i, _):
        rows = pl.ds(pl.multiple_of(i * 128, 128), 128)
        for part in range(kp // 128):
            lo, hi = spans[part]
            turned = lturn[part, rows, :]
            if hi - lo < 128:
                spot = lax.broadcasted_iota(jnp.int32, turned.shape, 1)
                turned = jnp.where(spot < hi - lo, turned, 0.0)
            lrows[rows, lo:lo + 128] = turned.astype(BF16)
        return 0

    lax.fori_loop(0, all_c * n // 128, pack_left, 0)

    def share_amps():
        for e in range(1, row_n):
            for i in range(pairs_of_cols):
                r, c = (row + e) % row_n, mate(i)
                arrival(t_block(r, c), t_recv.at[r * col_n + c])
                t3_copy(i, e).start()

    c_step = ybuf.shape[2] // width
    rows_c = c_step * n
    block_rows = slots * n
    early = ybuf.shape[0] > 1

    def take_amps():
        for e in range(row_n):
            for i in range(pairs_of_cols):
                r, c = (row + e) % row_n, 2 * ((cpair + i) % pairs_of_cols) + 1 - half
                arrival(t_block(r, c), t_recv.at[r * col_n + c])

        def turn_amps(i, _):
            for h in range(4):
                at = pl.multiple_of((4 * i + h) * width, width)
                tturn[pl.ds(at, width), :] = tbuf[4 * i + h].astype(F32).T.astype(BF16)
            return 0

        if early:
            lax.fori_loop(0, all_c // 4, turn_amps, 0)

    def s1_copy(step, e):
        r, k, slot = (row + e) % row_n, phase(step), step % 2
        return pltpu.make_async_remote_copy(
            src_ref=out1.at[slot, r], dst_ref=in1.at[k, row],
            send_sem=s1_send.at[slot * row_n + r], recv_sem=s1_recv.at[k * row_n + row],
            device_id=(r, col), device_id_type=MESH,
        )

    def land(step, r):
        k = phase(step)
        source = r * col_n + 2 * ((cpair + k) % pairs_of_cols)
        for x in range(2):
            share_arrival(rbuf.at[k, 2 * r + x], r_recv.at[source + x])

    def integrals(step, r, ci, lead, first_row):
        k = phase(step)
        at = pl.multiple_of(ci * rows_c, rows_c)
        weights = jnp.concatenate([rbuf[k, 2 * r], rbuf[k, 2 * r + 1]], axis=1)
        block = jnp.dot(
            lrows[pl.ds(at, rows_c), :], weights, preferred_element_type=F32
        ).astype(BF16).reshape(c_step, n, 2 * width)
        for x in range(2):
            spot = pl.ds(pl.multiple_of(first_row + (2 * r + x) * n, n), n)
            for c in range(c_step):
                ybuf[lead, spot, c * width:(c + 1) * width] = block[
                    c, :, x * width:(x + 1) * width
                ]

    def emit(step, first_row):
        @pl.when(step >= 2)
        def _():
            for e in range(1, row_n):
                s1_copy(step, e).wait_send()

        part = acc[pl.ds(first_row, block_rows), :].reshape(slots, row_n, a_own, all_p)
        for r in range(row_n):
            out1[step % 2, r] = part[:, r]
        for e in range(1, row_n):
            s1_copy(step, e).start()
        in1[phase(step), row] = out1[step % 2, row]

    def all_integrals(step, _):
        first_row = pl.multiple_of(step * block_rows, block_rows)

        def some_b(j, _):
            r = (row + row_n - j) % row_n
            land(step, r)

            def some_c(ci, _):
                integrals(step, r, ci, ci, first_row)
                return 0

            lax.fori_loop(0, all_c // c_step, some_c, 0)
            return 0

        lax.fori_loop(0, row_n, some_b, 0)
        return 0

    def ladder(first_row, rows):
        acc[pl.ds(0, rows), :] = jnp.zeros((rows, all_p), F32)

        def some_c(ci, _):
            depth = c_step * width
            at = pl.multiple_of(ci * depth, depth)
            acc[pl.ds(0, rows), :] += jnp.dot(
                ybuf[ci, pl.ds(first_row, rows), :], tturn[pl.ds(at, depth), :],
                preferred_element_type=F32,
            )
            return 0

        lax.fori_loop(0, all_c // c_step, some_c, 0)

    def chunk(step, _):
        acc[...] = jnp.zeros_like(acc)
        for r in range(row_n):
            land(step, r)

        def some_c(ci, _):
            def some_b(r, _):
                integrals(step, r, ci, 0, 0)
                return 0

            lax.fori_loop(0, row_n, some_b, 0)
            amp = jnp.concatenate([tbuf[c_step * ci + c] for c in range(c_step)], axis=1)
            acc[...] += lax.dot_general(
                ybuf[0], amp, (((1,), (1,)), ((), ())), preferred_element_type=F32
            )
            return 0

        lax.fori_loop(0, all_c // c_step, some_c, 0)
        emit(step, 0)
        return 0

    if early:
        all_integrals(0, 0)
        share_amps()
        all_integrals(1, 0)
        take_amps()
        ladder(0, 2 * block_rows)
        for step in range(2):
            emit(step, step * block_rows)

        def later(step, _):
            all_integrals(step, 0)
            ladder(pl.multiple_of(step * block_rows, block_rows), block_rows)
            emit(step, 0)
            return 0

        lax.fori_loop(2, pairs_of_cols, later, 0)
    else:
        share_amps()
        take_amps()
        lax.fori_loop(0, pairs_of_cols, chunk, 0)

    def gather_rows(step, _):
        k = phase(step)
        part = in1[k, row]
        for e in range(1, row_n):
            r = (row + e) % row_n
            arrival(in1.at[k, r], s1_recv.at[k * row_n + r])
            part += in1[k, r]
        source = 2 * ((cpair + k) % pairs_of_cols)
        for j in range(slots):
            b = (j // 2) * col_n + source + j % 2
            for x in range(all_p // 128):
                fin[x, pl.ds(b, a_own, stride=n), :] = part[j, :, x * 128:(x + 1) * 128]
        return 0

    lax.fori_loop(0, pairs_of_cols, gather_rows, 0)
    for x in range(all_p // 128):
        out2[x * 128:(x + 1) * 128, :] = fin[x].T

    def s2_copy(e):
        c = (col + e) % col_n
        return pltpu.make_async_remote_copy(
            src_ref=out2.at[pl.ds(c * pb, pb), :], dst_ref=in2.at[col],
            send_sem=s2_send.at[c], recv_sem=s2_recv.at[col],
            device_id=(row, c), device_id_type=MESH,
        )

    for e in range(1, col_n):
        s2_copy(e).start()
    total = out2[pl.ds(pl.multiple_of(col * pb, pb), pb), :]
    for e in range(1, col_n):
        c = (col + e) % col_n
        arrival(in2.at[c], s2_recv.at[c])
        total += in2[c]
    out[...] = (total / den[...]).astype(out.dtype)

    for i in range(len(hops)):
        t1_copy(i).wait_send()
    for i in range(pairs_of_cols):
        for e in range(row_n):
            if e > 0:
                t2_copy(i, e).wait_send()
            t3_copy(i, e).wait_send()

    for step in range(max(0, pairs_of_cols - 2), pairs_of_cols):
        for e in range(1, row_n):
            s1_copy(step, e).wait_send()

    def drain(e, _):
        d = (me + e) % n
        left_share(d, begun)
        right_share(0, d, begun)
        return 0

    lax.fori_loop(1, n, drain, 0)
    for e in range(1, col_n):
        s2_copy(e).wait_send()


def shards(panel_left, panel_right, amplitudes, eps_virtual, eps_occupied, pair_list, blocks):
    row_n = lax.axis_size("row")
    col_n = lax.axis_size("col")
    n = row_n * col_n
    fit, _, width = panel_left.shape
    pb, cb, _ = amplitudes.shape
    units = -(-fit // 16)
    base, extra = units // n, units % n
    kp = -(-16 * (base + 1) // 128) * 128
    left = panel_left.reshape(fit, width)
    right = panel_right.reshape(fit, width)
    last = 16 * (units - 1)
    tails = jnp.pad(jnp.stack([left[last:], right[last:]]), ((0, 0), (0, 16 * units - fit), (0, 0)))
    amps = jnp.transpose(amplitudes, (1, 0, 2))
    all_c, all_p = cb * row_n, pb * col_n
    halves = col_n // 2
    slots = 2 * row_n
    a_own = n // row_n
    span = n * a_own
    early = all_c * n * n * width <= 2 ** 24 and all_p <= width
    c_step = 32 if early else 2
    dma = pltpu.SemaphoreType.DMA
    hbm = pl.BlockSpec(memory_space=pl.ANY)
    smem = pl.BlockSpec(memory_space=pltpu.SMEM)
    flat = pl.pallas_call(
        functools.partial(kernel, row_n, col_n, base, extra),
        out_shape=jax.ShapeDtypeStruct((pb, span), BF16),
        in_specs=[hbm, hbm, hbm, hbm, smem, smem, smem, smem],
        out_specs=pl.BlockSpec(memory_space=pltpu.VMEM),
        scratch_shapes=[
            pltpu.VMEM((n, kp, width), BF16),
            pltpu.VMEM((halves, slots, kp, width), BF16),
            pltpu.VMEM((kp // 128, all_c * n, 128), F32),
            pltpu.VMEM((all_c * n, kp), BF16),
            pltpu.VMEM((all_c, all_p, width), BF16),
            pltpu.VMEM((all_c * width if early else 16, all_p), BF16),
            pltpu.VMEM(
                (all_c // c_step, n * n, c_step * width) if early else (1, slots * n, c_step * width),
                BF16,
            ),
            pltpu.VMEM((2 * slots * n if early else slots * n, all_p), F32),
            pltpu.VMEM((2, row_n, slots, a_own, all_p), F32),
            pltpu.VMEM((halves, row_n, slots, a_own, all_p), F32),
            pltpu.VMEM((all_p // 128, span, 128), F32),
            pltpu.VMEM((all_p, span), F32),
            pltpu.VMEM((col_n, pb, span), F32),
            pltpu.VMEM((pb, span), F32),
            dma((n,)), dma((n,)), dma((n,)), dma((n,)),
            dma((halves,)), dma((halves * row_n,)), dma((halves * row_n,)), dma((n,)),
            dma((2 * row_n,)), dma((halves * row_n,)), dma((col_n,)), dma((col_n,)),
        ],
        compiler_params=pltpu.CompilerParams(
            collective_id=0, has_side_effects=True, vmem_limit_bytes=62 * 1024 * 1024
        ),
        cost_estimate=pl.CostEstimate(
            flops=2 * fit * width * width * n, bytes_accessed=4 * fit * width, transcendentals=0
        ),
        name="ladder_exchange",
    )(left, right, tails, amps, eps_virtual, eps_occupied, pair_list.T, blocks)
    return flat.reshape(pb, a_own, n)


def solution(mesh):
    return jax.shard_map(
        shards,
        mesh=mesh,
        in_specs=(
            P(None, ("row", "col"), None),
            P(None, ("row", "col"), None),
            P("col", "row", None),
            P(),
            P(),
            P(),
            P(),
        ),
        out_specs=P("col", "row", None),
        check_vma=False,
    )
```

```python
import functools

import jax
import jax.numpy as jnp
from jax import lax
from jax.experimental import pallas as pl
from jax.experimental.pallas import tpu as pltpu
from jax.sharding import PartitionSpec as P

MESH = pl.DeviceIdType.MESH
F32 = jnp.float32
BF16 = jnp.bfloat16


def arrival(ref, sem):
    pltpu.make_async_copy(ref, ref, sem).wait()


def kernel(
    row_n, col_n, base, extra,
    left, right, tails, amps, eps_v, eps_o, pairs, blocks,
    out,
    lbuf, rbuf, lturn, lrows, tbuf, tturn, ybuf, acc, out1, in1, fin, out2, in2, den,
    l_send, l_recv, r_send, r_recv, t_send1, t_send2, t_send3, t_recv,
    s1_send, s1_recv, s2_send, s2_recv,
):
    n = row_n * col_n
    pairs_of_cols = col_n // 2
    slots = 2 * row_n
    cb, pb, width = amps.shape
    all_c = cb * row_n
    all_p = pb * col_n
    kp = lbuf.shape[1]
    few, most = 16 * base, 16 * (base + 1)
    a_own = n // row_n
    row = lax.axis_index("row")
    col = lax.axis_index("col")
    me = row * col_n + col
    cpair = col // 2
    half = col % 2

    barrier = pltpu.get_barrier_semaphore()

    def greet(e, _):
        d = (me + e) % n
        pl.semaphore_signal(barrier, inc=1, device_id=(d // col_n, d % col_n), device_id_type=MESH)
        return 0

    lax.fori_loop(1, n, greet, 0)

    def t_block(r, c):
        return tbuf.at[pl.ds(r * cb, cb), pl.ds(c * pb, pb), :]

    pltpu.make_async_copy(amps, t_block(row, col), t_recv.at[me]).start()

    def shares(src, which, dst, d, copy, act):
        @pl.when(d < extra)
        def _():
            act(copy(src.at[pl.ds(d * most, most), :], dst.at[pl.ds(0, most), :]))

        @pl.when((d >= extra) & (d < n - 1))
        def _():
            at = extra * most + (d - extra) * few
            act(copy(src.at[pl.ds(at, few), :], dst.at[pl.ds(0, few), :]))

        @pl.when(d == n - 1)
        def _():
            at = extra * most + (n - 1 - extra) * few
            act(copy(src.at[pl.ds(at, few - 16), :], dst.at[pl.ds(0, few - 16), :]))
            act(copy(tails.at[which], dst.at[pl.ds(few - 16, 16), :]))

    def share_arrival(ref, sem):
        @pl.when(me < extra)
        def _():
            arrival(ref.at[pl.ds(0, most), :], sem)

        @pl.when(me >= extra)
        def _():
            arrival(ref.at[pl.ds(0, few), :], sem)

    def begin(copy):
        copy.start()

    def begun(copy):
        copy.wait_send()

    shares(left, 0, lbuf.at[me], me, lambda a, b: pltpu.make_async_copy(a, b, l_recv.at[me]), begin)
    shares(
        right, 1, rbuf.at[0, row * 2 + half], me,
        lambda a, b: pltpu.make_async_copy(a, b, r_recv.at[me]), begin,
    )

    def clear(at):
        def one(i, _):
            lbuf[i, pl.ds(at, kp - at), :] = jnp.zeros((kp - at, width), BF16)
            rbuf[i // slots, i % slots, pl.ds(at, kp - at), :] = jnp.zeros((kp - at, width), BF16)
            return 0

        lax.fori_loop(0, n, one, 0)

    if kp > most:
        @pl.when(me < extra)
        def _():
            clear(most)

    @pl.when(me >= extra)
    def _():
        clear(few)

    pl.semaphore_wait(barrier, n - 1)

    def mate(i):
        other, bit = cpair, 1
        while bit <= i:
            if i & bit:
                other = other + bit * (1 - 2 * ((other // bit) % 2))
            bit *= 2
        return 2 * other + half

    hops, bit, held = [], pairs_of_cols // 2, [0]
    while bit:
        hops += [(block, bit) for block in held]
        held += [block + bit for block in held]
        bit //= 2

    def t1_copy(i):
        block, partner = hops[i]
        c = mate(block)
        return pltpu.make_async_remote_copy(
            src_ref=t_block(row, c), dst_ref=t_block(row, c),
            send_sem=t_send1.at[i], recv_sem=t_recv.at[row * col_n + c],
            device_id=(row, mate(partner)), device_id_type=MESH,
        )

    def t2_copy(i, e):
        c = mate(i)
        return pltpu.make_async_remote_copy(
            src_ref=t_block(row, c), dst_ref=t_block(row, c),
            send_sem=t_send2.at[i * row_n + e], recv_sem=t_recv.at[row * col_n + c],
            device_id=((row + e) % row_n, col), device_id_type=MESH,
        )

    def t3_copy(i, e):
        c, r = mate(i), (row + e) % row_n
        return pltpu.make_async_remote_copy(
            src_ref=t_block(r, c), dst_ref=t_block(r, c),
            send_sem=t_send3.at[i * row_n + e], recv_sem=t_recv.at[r * col_n + c],
            device_id=(row, 2 * cpair + 1 - half), device_id_type=MESH,
        )

    def target(k, j):
        to_row, to_half = (row + j // 2) % row_n, (half + j) % 2
        return to_row * col_n + 2 * ((cpair + pairs_of_cols - k) % pairs_of_cols) + to_half

    def remote(send, recv, d):
        return lambda a, b: pltpu.make_async_remote_copy(
            src_ref=a, dst_ref=b, send_sem=send.at[d], recv_sem=recv.at[me],
            device_id=(d // col_n, d % col_n), device_id_type=MESH,
        )

    def left_share(d, act):
        shares(left, 0, lbuf.at[me], d, remote(l_send, l_recv, d), act)

    def right_share(k, d, act):
        shares(right, 1, rbuf.at[k, row * 2 + half], d, remote(r_send, r_recv, d), act)

    def phase(step):
        return ((step + pairs_of_cols - 1) // pairs_of_cols) * (1 + step % (pairs_of_cols - 1))

    def send_left(j, _):
        def one(step, _):
            d = target(phase((step + 1) % pairs_of_cols), j)

            @pl.when(d != me)
            def _():
                left_share(d, begin)

            return 0

        lax.fori_loop(0, pairs_of_cols, one, 0)
        return 0

    def send_right(first, count, start, stop):
        def one(i, _):
            k = phase(first + i % count)
            d = target(k, i // count)

            @pl.when(d != me)
            def _():
                right_share(k, d, begin)

            return 0

        lax.fori_loop(count * start, count * stop, one, 0)

    here = set()

    def need(block):
        if block not in here:
            here.add(block)
            c = mate(block)
            arrival(t_block(row, c), t_recv.at[row * col_n + c])

    for own in (True, False):
        for i, (block, _) in enumerate(hops):
            if (block == 0) == own:
                need(block)
                t1_copy(i).start()
        if own:
            lax.fori_loop(0, slots // 4, send_left, 0)
    waiting = [(i, e) for i in range(pairs_of_cols) for e in range(1, row_n)]
    lefts = slots - slots // 4
    groups = lefts + slots // 2
    for g in range(groups):
        if g < lefts:
            send_left(slots // 4 + g, 0)
        else:
            send_right(0, 2, 2 * (g - lefts), 2 * (g - lefts) + 2)
        while len(waiting) * groups > (groups - 1 - g) * pairs_of_cols * (row_n - 1):
            i, e = waiting.pop(0)
            need(i)
            t2_copy(i, e).start()
    for step in range(2, pairs_of_cols):
        send_right(step, 1, 0, slots)

    span = n * a_own
    lane = lax.broadcasted_iota(jnp.int32, (pb, span), 1)
    line = lax.broadcasted_iota(jnp.int32, (pb, span), 0)
    first_at = blocks[0] * n + row * a_own
    second_at = blocks[1] * n
    first = jnp.zeros((pb, span), F32)
    for i in range(a_own):
        first = jnp.where(lane // n == i, eps_v[first_at + i], first)
    den[...] = first

    def add_second(b, _):
        den[...] = jnp.where(lane % n == b, den[...] + eps_v[second_at + b], den[...])
        return 0

    lax.fori_loop(0, n, add_second, 0)
    pair_sum = jnp.zeros((pb, span), F32)
    for i in range(pb):
        at = col * pb + i
        level = eps_o[pairs[0, at]] + eps_o[pairs[1, at]]
        pair_sum = jnp.where(line == i, level, pair_sum)
    den[...] = den[...] - pair_sum

    spans = [(lo, min(lo + 128, most)) for lo in range(0, kp, 128)]

    def turn_left(i, _):
        for x in range(4):
            share_arrival(lbuf.at[4 * i + x], l_recv.at[4 * i + x])
        flipped = [
            [lbuf[4 * i + x, lo:hi, :].astype(F32).T for lo, hi in spans] for x in range(4)
        ]
        for x in range(4):
            for part, (lo, hi) in enumerate(spans):
                lturn[part, pl.ds(4 * i + x, all_c, stride=n), :hi - lo] = flipped[x][part]
        return 0

    lax.fori_loop(0, n // 4, turn_left, 0)

    def pack_left(i, _):
        rows = pl.ds(pl.multiple_of(i * 128, 128), 128)
        for part in range(kp // 128):
            lo, hi = spans[part]
            turned = lturn[part, rows, :]
            if hi - lo < 128:
                spot = lax.broadcasted_iota(jnp.int32, turned.shape, 1)
                turned = jnp.where(spot < hi - lo, turned, 0.0)
            lrows[rows, lo:lo + 128] = turned.astype(BF16)
        return 0

    lax.fori_loop(0, all_c * n // 128, pack_left, 0)

    def share_amps():
        for e in range(row_n):
            for i in range(pairs_of_cols):
                r, c = (row + e) % row_n, mate(i)
                if e > 0:
                    arrival(t_block(r, c), t_recv.at[r * col_n + c])
                t3_copy(i, e).start()

    c_step = ybuf.shape[2] // width
    rows_c = c_step * n
    block_rows = slots * n
    early = ybuf.shape[0] > 1

    def take_amps():
        for e in range(row_n):
            for i in range(pairs_of_cols):
                r, c = (row + e) % row_n, 2 * ((cpair + i) % pairs_of_cols) + 1 - half
                arrival(t_block(r, c), t_recv.at[r * col_n + c])

        def turn_amps(i, _):
            for h in range(4):
                at = pl.multiple_of((4 * i + h) * width, width)
                tturn[pl.ds(at, width), :] = tbuf[4 * i + h].astype(F32).T.astype(BF16)
            return 0

        if early:
            lax.fori_loop(0, all_c // 4, turn_amps, 0)

    def s1_copy(step, e):
        r, k, slot = (row + e) % row_n, phase(step), step % 2
        return pltpu.make_async_remote_copy(
            src_ref=out1.at[slot, r], dst_ref=in1.at[k, row],
            send_sem=s1_send.at[slot * row_n + r], recv_sem=s1_recv.at[k * row_n + row],
            device_id=(r, col), device_id_type=MESH,
        )

    def land(step, r):
        k = phase(step)
        source = r * col_n + 2 * ((cpair + k) % pairs_of_cols)
        for x in range(2):
            share_arrival(rbuf.at[k, 2 * r + x], r_recv.at[source + x])

    def integrals(step, r, ci, lead, first_row):
        k = phase(step)
        at = pl.multiple_of(ci * rows_c, rows_c)
        weights = jnp.concatenate([rbuf[k, 2 * r], rbuf[k, 2 * r + 1]], axis=1)
        block = jnp.dot(
            lrows[pl.ds(at, rows_c), :], weights, preferred_element_type=F32
        ).astype(BF16).reshape(c_step, n, 2 * width)
        for x in range(2):
            spot = pl.ds(pl.multiple_of(first_row + (2 * r + x) * n, n), n)
            for c in range(c_step):
                ybuf[lead, spot, c * width:(c + 1) * width] = block[
                    c, :, x * width:(x + 1) * width
                ]

    def emit(step, first_row):
        @pl.when(step >= 2)
        def _():
            for e in range(1, row_n):
                s1_copy(step, e).wait_send()

        part = acc[pl.ds(first_row, block_rows), :].reshape(slots, row_n, a_own, all_p)
        for r in range(row_n):
            out1[step % 2, r] = part[:, r]
        for e in range(1, row_n):
            s1_copy(step, e).start()
        in1[phase(step), row] = out1[step % 2, row]

    def all_integrals(step, _):
        first_row = pl.multiple_of(step * block_rows, block_rows)

        def some_b(j, _):
            r = (row + row_n - j) % row_n
            land(step, r)

            def some_c(ci, _):
                integrals(step, r, ci, ci, first_row)
                return 0

            lax.fori_loop(0, all_c // c_step, some_c, 0)
            return 0

        lax.fori_loop(0, row_n, some_b, 0)
        return 0

    def ladder(first_row, rows):
        acc[pl.ds(0, rows), :] = jnp.zeros((rows, all_p), F32)

        def some_c(ci, _):
            depth = c_step * width
            at = pl.multiple_of(ci * depth, depth)
            acc[pl.ds(0, rows), :] += jnp.dot(
                ybuf[ci, pl.ds(first_row, rows), :], tturn[pl.ds(at, depth), :],
                preferred_element_type=F32,
            )
            return 0

        lax.fori_loop(0, all_c // c_step, some_c, 0)

    def chunk(step, _):
        acc[...] = jnp.zeros_like(acc)
        for r in range(row_n):
            land(step, r)

        def some_c(ci, _):
            def some_b(r, _):
                integrals(step, r, ci, 0, 0)
                return 0

            lax.fori_loop(0, row_n, some_b, 0)
            amp = jnp.concatenate([tbuf[c_step * ci + c] for c in range(c_step)], axis=1)
            acc[...] += lax.dot_general(
                ybuf[0], amp, (((1,), (1,)), ((), ())), preferred_element_type=F32
            )
            return 0

        lax.fori_loop(0, all_c // c_step, some_c, 0)
        emit(step, 0)
        return 0

    if early:
        all_integrals(0, 0)
        share_amps()
        all_integrals(1, 0)
        take_amps()
        ladder(0, 2 * block_rows)
        for step in range(2):
            emit(step, step * block_rows)

        def later(step, _):
            all_integrals(step, 0)
            ladder(pl.multiple_of(step * block_rows, block_rows), block_rows)
            emit(step, 0)
            return 0

        lax.fori_loop(2, pairs_of_cols, later, 0)
    else:
        share_amps()
        take_amps()
        lax.fori_loop(0, pairs_of_cols, chunk, 0)

    def gather_rows(step, _):
        k = phase(step)
        part = in1[k, row]
        for e in range(1, row_n):
            r = (row + e) % row_n
            arrival(in1.at[k, r], s1_recv.at[k * row_n + r])
            part += in1[k, r]
        source = 2 * ((cpair + k) % pairs_of_cols)
        for j in range(slots):
            b = (j // 2) * col_n + source + j % 2
            for x in range(all_p // 128):
                fin[x, pl.ds(b, a_own, stride=n), :] = part[j, :, x * 128:(x + 1) * 128]
        return 0

    lax.fori_loop(0, pairs_of_cols, gather_rows, 0)
    for x in range(all_p // 128):
        out2[x * 128:(x + 1) * 128, :] = fin[x].T

    def s2_copy(e):
        c = (col + e) % col_n
        return pltpu.make_async_remote_copy(
            src_ref=out2.at[pl.ds(c * pb, pb), :], dst_ref=in2.at[col],
            send_sem=s2_send.at[c], recv_sem=s2_recv.at[col],
            device_id=(row, c), device_id_type=MESH,
        )

    for e in range(1, col_n):
        s2_copy(e).start()
    total = out2[pl.ds(pl.multiple_of(col * pb, pb), pb), :]
    for e in range(1, col_n):
        c = (col + e) % col_n
        arrival(in2.at[c], s2_recv.at[c])
        total += in2[c]
    out[...] = (total / den[...]).astype(out.dtype)

    for i in range(len(hops)):
        t1_copy(i).wait_send()
    for i in range(pairs_of_cols):
        for e in range(row_n):
            if e > 0:
                t2_copy(i, e).wait_send()
            t3_copy(i, e).wait_send()

    for step in range(max(0, pairs_of_cols - 2), pairs_of_cols):
        for e in range(1, row_n):
            s1_copy(step, e).wait_send()

    def drain(e, _):
        d = (me + e) % n
        left_share(d, begun)
        right_share(0, d, begun)
        return 0

    lax.fori_loop(1, n, drain, 0)
    for e in range(1, col_n):
        s2_copy(e).wait_send()


def shards(panel_left, panel_right, amplitudes, eps_virtual, eps_occupied, pair_list, blocks):
    row_n = lax.axis_size("row")
    col_n = lax.axis_size("col")
    n = row_n * col_n
    fit, _, width = panel_left.shape
    pb, cb, _ = amplitudes.shape
    units = -(-fit // 16)
    base, extra = units // n, units % n
    kp = -(-16 * (base + 1) // 128) * 128
    left = panel_left.reshape(fit, width)
    right = panel_right.reshape(fit, width)
    last = 16 * (units - 1)
    tails = jnp.pad(jnp.stack([left[last:], right[last:]]), ((0, 0), (0, 16 * units - fit), (0, 0)))
    amps = jnp.transpose(amplitudes, (1, 0, 2))
    all_c, all_p = cb * row_n, pb * col_n
    halves = col_n // 2
    slots = 2 * row_n
    a_own = n // row_n
    span = n * a_own
    early = all_c * n * n * width <= 2 ** 24 and all_p <= width
    c_step = 32 if early else 2
    dma = pltpu.SemaphoreType.DMA
    hbm = pl.BlockSpec(memory_space=pl.ANY)
    smem = pl.BlockSpec(memory_space=pltpu.SMEM)
    flat = pl.pallas_call(
        functools.partial(kernel, row_n, col_n, base, extra),
        out_shape=jax.ShapeDtypeStruct((pb, span), BF16),
        in_specs=[hbm, hbm, hbm, hbm, smem, smem, smem, smem],
        out_specs=pl.BlockSpec(memory_space=pltpu.VMEM),
        scratch_shapes=[
            pltpu.VMEM((n, kp, width), BF16),
            pltpu.VMEM((halves, slots, kp, width), BF16),
            pltpu.VMEM((kp // 128, all_c * n, 128), F32),
            pltpu.VMEM((all_c * n, kp), BF16),
            pltpu.VMEM((all_c, all_p, width), BF16),
            pltpu.VMEM((all_c * width if early else 16, all_p), BF16),
            pltpu.VMEM(
                (all_c // c_step, n * n, c_step * width) if early else (1, slots * n, c_step * width),
                BF16,
            ),
            pltpu.VMEM((2 * slots * n if early else slots * n, all_p), F32),
            pltpu.VMEM((2, row_n, slots, a_own, all_p), F32),
            pltpu.VMEM((halves, row_n, slots, a_own, all_p), F32),
            pltpu.VMEM((all_p // 128, span, 128), F32),
            pltpu.VMEM((all_p, span), F32),
            pltpu.VMEM((col_n, pb, span), F32),
            pltpu.VMEM((pb, span), F32),
            dma((n,)), dma((n,)), dma((n,)), dma((n,)),
            dma((halves,)), dma((halves * row_n,)), dma((halves * row_n,)), dma((n,)),
            dma((2 * row_n,)), dma((halves * row_n,)), dma((col_n,)), dma((col_n,)),
        ],
        compiler_params=pltpu.CompilerParams(
            collective_id=0, has_side_effects=True, vmem_limit_bytes=62 * 1024 * 1024
        ),
        cost_estimate=pl.CostEstimate(
            flops=2 * fit * width * width * n, bytes_accessed=4 * fit * width, transcendentals=0
        ),
        name="ladder_exchange",
    )(left, right, tails, amps, eps_virtual, eps_occupied, pair_list.T, blocks)
    return flat.reshape(pb, a_own, n)


def solution(mesh):
    return jax.shard_map(
        shards,
        mesh=mesh,
        in_specs=(
            P(None, ("row", "col"), None),
            P(None, ("row", "col"), None),
            P("col", "row", None),
            P(),
            P(),
            P(),
            P(),
        ),
        out_specs=P("col", "row", None),
        check_vma=False,
    )
```
